256 devices in a mesh: gx: 32 (over z, x), gy: 8 (over y, core).
Axes of the slice: x: 4, y: 4, z: 8, core: 2. Of those that a mesh axis runs over, the one named last changes fastest.
Arguments:
- source_field: float32 [3, 8, 128, 64, 128], P(None, None, 'gx', 'gy'), may hold values from -50 to 50
- density_class: int32 [128, 64, 128], P('gx', 'gy'), may hold values from 0 to 15
- fixed_mask: int32 [128, 64, 128], P('gx', 'gy'), may hold values 0 or 1
- load_nodes: int32 [8, 64], replicated, may hold values from 0 to 1048575, as said below
- load_forces: float32 [3, 8, 64], replicated, may hold values from -16 to 16
Outputs:
- solution: float32 [3, 8, 128, 64, 128], P(None, None, 'gx', 'gy')
- residual: float32 [3, 8, 128, 64, 128], P(None, None, 'gx', 'gy')
The draws below stay inside these ranges and needn't reach their ends.
Inputs may be any that keep to these rules, and one draw needn't show every extreme that they name: `load_nodes`: each entry is the index (x * 64 + y) * 128 + z of a voxel of the whole grid; repeats may occur.
All inputs are finite; a program needn't handle non-finite values. No bound on the sum of `fixed_mask` on one device may be relied on, other than what follows from the above.
Results may differ from the reference program's by a relative error of at most 0.0003.
Values sent between devices are 32-bit elements; how exact they have to be, the bound alone decides.
A program may use at most 128 MiB of HBM per device.

```python
import math
import jax
import jax.numpy as jnp
from jax import lax

NZ = 128
CASES = 8
LOADS = 64
CLASSES = 16
LEVELS = 3
ITERS = 2
NX = 128
NY = 64
NODES = 1048576


def draw_source_field(key, part):
    key = jax.random.fold_in(key, 11)
    key_base, key_plane, key_case = jax.random.split(key, 3)
    plane_scale = jnp.exp(jax.random.uniform(key_plane, (NX,), jnp.float32) * math.log(10.0))
    case_scale = jnp.exp(jax.random.uniform(key_case, (CASES,), jnp.float32) * math.log(10.0))
    scale = 0.1 * case_scale[None, :, None, None, None] * plane_scale[None, None, :, None, None]
    values = jnp.clip(jax.random.normal(key_base, (3, CASES, NX, NY, NZ), jnp.float32), -5.0, 5.0)
    return (scale * values).astype(jnp.float32)


def draw_load_nodes(key, part):
    key = jax.random.fold_in(key, 23)
    nodes = jax.random.randint(key, (CASES, LOADS), 0, NODES, dtype=jnp.int32)
    nodes = nodes.at[0, 0].set(0)
    nodes = nodes.at[0, 1].set(NODES - 1)
    return nodes


def place_ends(drawn, own_key, low, largest):
    longest = drawn.shape.index(max(drawn.shape))
    spots = []
    for shift in (0, 1):
        where = [jax.random.randint(jax.random.fold_in(own_key, axis), (), 0, length) for axis, length in enumerate(drawn.shape)]
        where[longest] = (where[longest] + shift) % drawn.shape[longest]
        spots.append(tuple(where))
    return drawn.at[spots[0]].set(low).at[spots[1]].set(largest)


def gaussian(rng, dims, deviation, reach, kind=jnp.bfloat16):
    entries = deviation * jax.random.normal(rng, dims, jnp.float32)
    return jnp.clip(entries, min=-reach, max=reach).astype(kind)


def setup_inputs(seed: int = 0) -> dict:
    arg_keys = jax.random.split(jax.random.key(seed), 6)
    source_field = draw_source_field(jax.random.fold_in(arg_keys[5], 71), 0)
    density_class = place_ends(jax.random.randint(arg_keys[1], (NX, NY, NZ), 0, CLASSES), jax.random.fold_in(arg_keys[1], 1), 0, CLASSES - 1).astype(jnp.int32)
    fixed_mask = place_ends((jax.random.randint(arg_keys[2], (NX, NY, NZ), 0, 16) < 1).astype(jnp.int32), jax.random.fold_in(arg_keys[2], 1), 0, 1)
    load_nodes = draw_load_nodes(jax.random.fold_in(arg_keys[5], 71), 0)
    load_forces = gaussian(arg_keys[4], (3, CASES, LOADS), 4.0, 16.0, jnp.float32)
    return {"source_field": source_field, "density_class": density_class, "fixed_mask": fixed_mask, "load_nodes": load_nodes, "load_forces": load_forces}


SHEAR_MODULUS = 1.0 / 2.6
LAME_FIRST = 0.3 / 0.52
MIN_MODULUS = 0.05
STEP_FIRST = 1.0 / (2.7 + 2.1 * math.cos(math.pi / 4.0))
STEP_SECOND = 1.0 / (2.7 - 2.1 * math.cos(math.pi / 4.0))

def crop_box(array, starts, lengths):
    return array[..., starts[0]:starts[0] + lengths[0], starts[1]:starts[1] + lengths[1], starts[2]:starts[2] + lengths[2]]

def offset_along(axis_d, moved, rest):
    return tuple((moved if k == axis_d else rest for k in range(3)))

def stiffness(padded, modulus):
    shape_now = padded.shape[-3:]
    inside_len = tuple((s - 2 for s in shape_now))
    outer_len = tuple((s - 1 for s in shape_now))
    middle = crop_box(padded, (1, 1, 1), inside_len)
    middle_mod = crop_box(modulus, (1, 1, 1), inside_len)
    laplacian = jnp.zeros_like(middle)
    for d in range(3):
        lower_box = offset_along(d, 0, 1)
        upper_box = offset_along(d, 2, 1)
        laplacian = laplacian + (crop_box(modulus, lower_box, inside_len) + middle_mod) * (middle - crop_box(padded, lower_box, inside_len))
        laplacian = laplacian + (middle_mod + crop_box(modulus, upper_box, inside_len)) * (middle - crop_box(padded, upper_box, inside_len))
    spread_sum = crop_box(padded[0], (1, 0, 0), outer_len) - crop_box(padded[0], (0, 0, 0), outer_len)
    for d in (1, 2):
        spread_sum = spread_sum + crop_box(padded[d], offset_along(d, 1, 0), outer_len) - crop_box(padded[d], (0, 0, 0), outer_len)
    flux_field = LAME_FIRST * crop_box(modulus, (0, 0, 0), outer_len) * spread_sum
    pieces = [crop_box(flux_field, offset_along(c, 0, 1), inside_len) - crop_box(flux_field, (1, 1, 1), inside_len) for c in range(3)]
    return 0.5 * SHEAR_MODULUS * laplacian + jnp.stack(pieces)

def diagonal_inverse(modpad, free):
    inside_len = tuple((s - 2 for s in modpad.shape))
    middle_mod = crop_box(modpad, (1, 1, 1), inside_len)
    total = jnp.zeros_like(middle_mod)
    for d in range(3):
        total = total + crop_box(modpad, offset_along(d, 0, 1), inside_len) + 2.0 * middle_mod + crop_box(modpad, offset_along(d, 2, 1), inside_len)
    rows = [0.5 * SHEAR_MODULUS * total + LAME_FIRST * (middle_mod + crop_box(modpad, offset_along(c, 0, 1), inside_len)) for c in range(3)]
    diagonal = jnp.stack(rows)
    return (free / diagonal + (1.0 - free))[:, None]

def restrict_sum(field):
    lead = field.shape[:-3]
    extent = field.shape[-3:]
    shaped = field.reshape(lead + (extent[0] // 2, 2, extent[1] // 2, 2, extent[2] // 2, 2))
    return jnp.sum(shaped, axis=(-5, -3, -1))

def prolong(field):
    lead = field.shape[:-3]
    extent = field.shape[-3:]
    expanded = field[..., :, None, :, None, :, None]
    wide = jnp.broadcast_to(expanded, lead + (extent[0], 2, extent[1], 2, extent[2], 2))
    return wide.reshape(lead + (2 * extent[0], 2 * extent[1], 2 * extent[2]))

def apply_level(field, section):
    modpad, free, dinv = section
    padded = jnp.pad(free * field, ((0, 0), (0, 0), (1, 1), (1, 1), (1, 1)))
    return free * stiffness(padded, modpad) + (1.0 - free) * field

def plain_presmooth(rhs, section):
    dinv = section[2]
    current = STEP_FIRST * dinv * rhs
    remain = rhs - apply_level(current, section)
    current = current + STEP_SECOND * dinv * remain
    remain = rhs - apply_level(current, section)
    return (current, remain)

def vcycle(rhs, levels, level):
    section = levels[level]
    dinv = section[2]
    if level == len(levels) - 1:
        current = STEP_FIRST * dinv * rhs
        return current + STEP_SECOND * dinv * (rhs - apply_level(current, section))
    current, remain = plain_presmooth(rhs, section)
    coarse = vcycle(restrict_sum(remain), levels, level + 1)
    current = current + section[1] * prolong(coarse)
    current = current + STEP_SECOND * dinv * (rhs - apply_level(current, section))
    current = current + STEP_FIRST * dinv * (rhs - apply_level(current, section))
    return current

def gram_matrix(left, right):
    return jnp.einsum('cixyz,cjxyz->ij', left, right, precision=lax.Precision.HIGHEST)

def combine_cases(field, matrix):
    return jnp.einsum('cixyz,ij->cjxyz', field, matrix, precision=lax.Precision.HIGHEST)

def solve_small(matrix, rhs):
    factor = jnp.linalg.cholesky(matrix)
    middle = lax.linalg.triangular_solve(factor, rhs, left_side=True, lower=True)
    return lax.linalg.triangular_solve(factor, middle, left_side=True, lower=True, transpose_a=True)

def reference(source_field, density_class, fixed_mask, load_nodes, load_forces):
    relative = (density_class.astype(jnp.float32) + 1.0) / CLASSES
    modulus = MIN_MODULUS + (1.0 - MIN_MODULUS) * relative * relative * relative
    free = 1.0 - fixed_mask.astype(jnp.float32)
    levels = []
    for level in range(LEVELS):
        if level > 0:
            modulus = 0.25 * restrict_sum(modulus)
            free = jnp.ones_like(modulus)
        modpad = jnp.pad(modulus, 1)
        levels.append((modpad, free, diagonal_inverse(modpad, free)))
    flat = source_field.reshape(3, CASES, -1)
    case_ids = jnp.broadcast_to(jnp.arange(CASES, dtype=jnp.int32)[:, None], (CASES, LOADS))
    flat = flat.at[:, case_ids, load_nodes.astype(jnp.int32)].add(load_forces)
    right = levels[0][1] * flat.reshape(source_field.shape)
    solution = jnp.zeros_like(right)
    residual = right
    precond = vcycle(residual, levels, 0)
    search = precond
    rz_gram = gram_matrix(residual, precond)
    for step in range(ITERS):
        image = apply_level(search, levels[0])
        alpha = solve_small(gram_matrix(search, image), rz_gram)
        solution = solution + combine_cases(search, alpha)
        residual = residual - combine_cases(image, alpha)
        if step + 1 < ITERS:
            precond = vcycle(residual, levels, 0)
            rz_next = gram_matrix(residual, precond)
            beta = solve_small(rz_gram, rz_next)
            search = precond + combine_cases(search, beta)
            rz_gram = rz_next
    return (solution, residual)
```

```python
import functools
import math

import jax
import jax.numpy as jnp
from jax import lax
from jax.experimental import pallas as pl
from jax.experimental.pallas import tpu as pltpu
from jax.sharding import PartitionSpec as P

CLASSES = 16
MU = 1.0 / 2.6
LAM = 0.3 / 0.52
MIN_MODULUS = 0.05
STEP_A = 1.0 / (2.7 + 2.1 * math.cos(math.pi / 4.0))
STEP_B = 1.0 / (2.7 - 2.1 * math.cos(math.pi / 4.0))
MESH = pl.DeviceIdType.MESH
F32 = jnp.float32

NX, NY, NC, NZ, LOADS = 4, 8, 8, 128, 64
H = 3
AX, AY = NX + 2 * H, NY + 2 * H
N8 = [(1, 0), (-1, 0), (0, 1), (0, -1), (1, 1), (1, -1), (-1, 1), (-1, -1)]
N14 = [(dx, dy) for dx in (1, -1, 2, -2, 0) for dy in (0, 1, -1) if (dx, dy) != (0, 0)]

K_E, K_F, K_E2, K_G, K_X2, K_G2, K_X2C, K_G3, K_EC = 0, 1, 2, 3, 5, 7, 9, 11, 13
KINDS = 15


def lanes():
    return lax.broadcasted_iota(jnp.int32, (NC, NZ), 1)


def subl():
    return lax.broadcasted_iota(jnp.int32, (NC, NZ), 0)


def up(v, s):
    return pltpu.roll(v, NZ - s, 1)


def down(v, s):
    return pltpu.roll(v, s, 1)


def pair_sum(v, s):
    other = jnp.where((lanes() & s) == 0, up(v, s), down(v, s))
    return v + other


def row(v):
    return jnp.broadcast_to(v, (NC, NZ))


def span(d, n, h, base):
    if d > 0:
        return n - h, base - h, h
    if d < 0:
        return 0, base + n, h
    return 0, base, n


def coefficients(s, e_at, f_at, low, mid, inv, co):
    kx, ky, kzp, kzm, dm, cw, cf, ff, ad, bd = co
    last = lanes() >= NZ - s
    first = lanes() < s
    half = 0.5 * MU

    def lower(i, carry):
        for j in range(*low[1]):
            e, f = e_at(i, j), f_at(i, j)
            fx, fy = f_at(i + 1, j), f_at(i, j + 1)
            fzp = jnp.where(last, 0.0, up(f, s))
            fzm = jnp.where(first, 0.0, down(f, s))
            ezp, ezm = up(e, s), down(e, s)
            kx[i, j] = half * (e + e_at(i + 1, j)) * f * fx
            ky[i, j] = half * (e + e_at(i, j + 1)) * f * fy
            kzp[i, j] = half * (e + ezp) * f * fzp
            kzm[i, j] = half * (ezm + e) * f * fzm
            le = LAM * e
            cw[0, i, j] = le * fx
            cw[1, i, j] = le * fy
            cw[2, i, j] = le * fzp
            cf[i, j] = le * f
            ff[i, j] = f
        return carry

    lax.fori_loop(low[0][0], low[0][1], lower, 0)

    def total(i, j):
        e = e_at(i, j)
        ezp = jnp.where(last, 0.0, up(e, s))
        ezm = jnp.where(first, 0.0, down(e, s))
        ex, ey = e_at(i - 1, j), e_at(i, j - 1)
        d = half * (ex + e_at(i + 1, j) + ey + e_at(i, j + 1) + ezm + ezp + 6.0 * e)
        return e, (ex, ey, ezm), d

    def middle(i, carry):
        for j in range(*mid[1]):
            f = f_at(i, j)
            _, _, d = total(i, j)
            dm[i, j] = f * d + (1.0 - f)
        return carry

    lax.fori_loop(mid[0][0], mid[0][1], middle, 0)

    def smoother(i, carry):
        for j in range(*inv[1]):
            f = f_at(i, j)
            e, below, d = total(i, j)
            for c in range(3):
                diag = jnp.where(e > 0.0, d + LAM * (e + below[c]), 1.0)
                dinv = jnp.where(e > 0.0, f / diag + (1.0 - f), 0.0)
                ad[c, i, j] = STEP_A * dinv
                bd[c, i, j] = STEP_B * dinv
        return carry

    lax.fori_loop(inv[0][0], inv[0][1], smoother, 0)


def divergence(v, s, xr, yr, co, w):
    cw, cf = co[5], co[6]

    def body(i, carry):
        for j in range(yr[0] - 1, yr[1]):
            a, b, c = v[0, i, j], v[1, i, j], v[2, i, j]
            w[i, j] = (
                cw[0, i, j] * v[0, i + 1, j]
                + cw[1, i, j] * v[1, i, j + 1]
                + cw[2, i, j] * up(c, s)
                - cf[i, j] * (a + b + c)
            )
        return carry

    lax.fori_loop(xr[0] - 1, xr[1], body, 0)


def plane(v, s, i, j, co, w, wmask):
    kx, ky, kzp, kzm, dm, _, _, ff = co[:8]
    wc = w[i, j]
    wz = jnp.where(wmask, 0.0, down(wc, s))
    below = (w[i - 1, j], w[i, j - 1], wz)
    f = ff[i, j]
    k = (kx[i, j], kx[i - 1, j], ky[i, j], ky[i, j - 1], kzp[i, j], kzm[i, j])
    out = []
    for c in range(3):
        vc = v[c, i, j]
        lap = dm[i, j] * vc
        lap -= k[0] * v[c, i + 1, j] + k[1] * v[c, i - 1, j]
        lap -= k[2] * v[c, i, j + 1] + k[3] * v[c, i, j - 1]
        lap -= k[4] * up(vc, s) + k[5] * down(vc, s)
        out.append((vc, lap + f * (below[c] - wc)))
    return out


def apply(v, s, xr, yr, co, w, emit):
    divergence(v, s, xr, yr, co, w)
    wmask = lanes() < s

    def body(i, carry):
        for j in range(*yr):
            for c, (vc, av) in enumerate(plane(v, s, i, j, co, w, wmask)):
                emit(c, i, j, vc, av)
        return carry

    lax.fori_loop(xr[0], xr[1], body, 0)


def smooth(v, s, xr, yr, co, w, rhs, step, out):
    def emit(c, i, j, vc, av):
        out[c, i, j] = vc + step[c, i, j] * (rhs[c, i, j] - av)

    apply(v, s, xr, yr, co, w, emit)


def restrict(v, s, xr, yr, co, w, rhs, coarse):
    divergence(v, s, xr, yr, co, w)
    wmask = lanes() < s

    def body(q, carry):
        for y2 in range((yr[1] - yr[0]) // 2):
            acc = [None] * 3
            for a in range(2):
                for b in range(2):
                    i, j = xr[0] + 2 * q + a, yr[0] + 2 * y2 + b
                    for c, (_, av) in enumerate(plane(v, s, i, j, co, w, wmask)):
                        rem = rhs[c, i, j] - av
                        acc[c] = rem if acc[c] is None else acc[c] + rem
            for c in range(3):
                coarse[c, q, y2] = pair_sum(acc[c], s)
        return carry

    lax.fori_loop(0, (xr[1] - xr[0]) // 2, body, 0)


def column(m, i):
    picked = jnp.where(lanes() == subl(), row(m[i : i + 1, :]), 0.0)
    return row(jnp.sum(picked, axis=1, keepdims=True))


def mm(a, b):
    return sum(row(a[:, k : k + 1]) * row(b[k : k + 1, :]) for k in range(NC))


def mtm(a, b):
    return sum(column(a, k) * row(b[k : k + 1, :]) for k in range(NC))


def solve(matrix, rhs):
    aug = jnp.where(lanes() < NC, matrix, pltpu.roll(rhs, NC, 1))
    for k in range(NC):
        scaled = row(aug[k : k + 1, :]) / row(aug[k : k + 1, k : k + 1])
        aug = jnp.where(subl() == k, scaled, aug - row(aug[:, k : k + 1]) * scaled)
    return up(aug, NC)


def kernel(
    size_x, size_y,
    src, dens, mask, nodes, forces, xo, ro,
    eb, fb, e2b, ex, fx, e2x, e3x, one,
    g, pv, a1, a2, a3, a4, xb, w, loadbuf,
    kx, ky, kzp, kzm, dm, cw, cf, ff, ad, bd,
    kx2, ky2, kzp2, kzm2, dm2, cw2, cf2, ff2, ad2, bd2,
    kx3, ky3, kzp3, kzm3, dm3, cw3, cf3, ff3, ad3, bd3,
    t2, g2r, x2r, ecr, g2u, b1, b2, b3, b4, w2, e2u,
    t3, g3r, g3u, c1, c2, w3,
    gram, ps1, ps2, mats, raw,
    send, recv, psend, precv,
):
    gx, gy = lax.axis_index("gx"), lax.axis_index("gy")
    co1 = (kx, ky, kzp, kzm, dm, cw, cf, ff, ad, bd)
    co2 = (kx2, ky2, kzp2, kzm2, dm2, cw2, cf2, ff2, ad2, bd2)
    co3 = (kx3, ky3, kzp3, kzm3, dm3, cw3, cf3, ff3, ad3, bd3)
    even = (lanes() & 1) == 0
    low2 = (lanes() & 2) == 0

    def valid(dx, dy):
        return (gx + dx >= 0) & (gx + dx < size_x) & (gy + dy >= 0) & (gy + dy < size_y)

    def message(kind, k, d, refs):
        a, b = refs(*d)
        return pltpu.make_async_remote_copy(
            src_ref=a, dst_ref=b, send_sem=send.at[kind, k], recv_sem=recv.at[kind, k],
            device_id=(gx + d[0], gy + d[1]), device_id_type=MESH,
        )

    def start(kind, group, refs):
        for k, d in enumerate(group):
            @pl.when(valid(*d))
            def _():
                message(kind, k, d, refs).start()

    def arrive(kind, group, refs):
        for k, d in enumerate(group):
            @pl.when(valid(-d[0], -d[1]))
            def _():
                message(kind, k, d, refs).wait_recv()

    def sent(kind, group, refs):
        for k, d in enumerate(group):
            @pl.when(valid(*d))
            def _():
                message(kind, k, d, refs).wait_send()

    def boxes(ref):
        return lambda dx, dy: (ref.at[1, 1], ref.at[1 - dx, 1 - dy])

    def e2_refs(dx, dy):
        return e2b.at[2, 1], e2b.at[2 - dx, 1 - dy]

    def halo(source, target, h):
        def refs(dx, dy):
            sx, tx, nx = span(dx, NX, h, H)
            sy, ty, ny = span(dy, NY, h, H)
            a = source.at[:, pl.ds(H + sx, nx), pl.ds(H + sy, ny)]
            return a, target.at[:, pl.ds(tx, nx), pl.ds(ty, ny)]
        return refs

    def coarse_refs(ref):
        def refs(dx, dy):
            sy, ty, ny = span(dy, 4, 2, 2)
            return ref.at[:, 1, pl.ds(2 + sy, ny)], ref.at[:, 1 - dx, pl.ds(ty, ny)]
        return refs

    def g3_refs(ref):
        return lambda dx, dy: (ref.at[:, 2, 1], ref.at[:, 2 - dx, 1 - dy])

    zero3 = jnp.zeros((NX, NY, NZ), F32)
    for bx in range(3):
        for by in range(3):
            eb[bx, by] = zero3
            fb[bx, by] = zero3
    for bx in range(5):
        for by in range(3):
            e2b[bx, by] = jnp.zeros((NC, NZ), F32)
    for x in range(NX):
        rel = (dens[x].astype(F32) + 1.0) / CLASSES
        eb[1, 1, x] = MIN_MODULUS + (1.0 - MIN_MODULUS) * rel * rel * rel
        fb[1, 1, x] = 1.0 - mask[x].astype(F32)
    halves = []
    for q in range(2):
        t = eb[1, 1, 2 * q] + eb[1, 1, 2 * q + 1]
        halves.append(0.25 * pair_sum(t + pltpu.roll(t, NY - 1, 0), 1))
    e2b[2, 1] = jnp.where((subl() & 1) == 0, halves[0], pltpu.roll(halves[1], 1, 0))

    for c in range(3):
        for x in range(NX):
            for y in range(NY):
                raw[c, H + x, H + y] = src[pl.ds((c * NC * NX + x) * NY + y, NC, stride=NX * NY), :]

    bar = pltpu.get_barrier_semaphore()
    corners = [(dx, dy) for dx in (1, -1, 2, -2) for dy in (1, -1)]
    peers = jnp.int32(size_x + size_y - 2)

    def greet_x(d, carry):
        pl.semaphore_signal(bar, inc=1, device_id=(lax.rem(gx + d, size_x), gy), device_id_type=MESH)
        return carry

    def greet_y(d, carry):
        pl.semaphore_signal(bar, inc=1, device_id=(gx, lax.rem(gy + d, size_y)), device_id_type=MESH)
        return carry

    lax.fori_loop(1, size_x, greet_x, 0)
    lax.fori_loop(1, size_y, greet_y, 0)
    for d in corners:
        peers = peers + jnp.where(valid(*d), 1, 0)

        @pl.when(valid(*d))
        def _():
            pl.semaphore_signal(bar, inc=1, device_id=(gx + d[0], gy + d[1]), device_id_type=MESH)
    pl.semaphore_wait(bar, peers)

    start(K_E, N8, boxes(eb))
    start(K_F, N8, boxes(fb))
    start(K_G, N8, halo(raw, raw, 2))
    start(K_E2, N14, e2_refs)

    def load_case(i, carry):
        node = nodes[pl.ds(i, 1), :]
        nz = lax.rem(node, NZ)
        nyx = lax.div(node, NZ)
        ny = lax.rem(nyx, size_y * NY) - gy * NY + 2
        nx = lax.div(nyx, size_y * NY) - gx * NX + 2
        hot = jnp.where(lax.broadcasted_iota(jnp.int32, (NZ, LOADS), 0) == nz, 1.0, 0.0)
        rows = lax.broadcasted_iota(jnp.int32, (16, LOADS), 0)
        parts = []
        for c in range(3):
            force = forces[c, pl.ds(i, 1), :]
            for x in range(8):
                parts.append(jnp.where((rows == ny) & (nx == x), force, 0.0))
        got = lax.dot_general(
            jnp.concatenate(parts, axis=0), hot, (((1,), (1,)), ((), ())),
            precision=lax.Precision.HIGHEST, preferred_element_type=F32,
        )
        for k in range(24):
            loadbuf[pl.ds(k * 96 + i, 8, stride=NC), :] = got[16 * k : 16 * k + 8]
            loadbuf[pl.ds(k * 96 + 64 + i, 4, stride=NC), :] = got[16 * k + 8 : 16 * k + 12]
        return carry

    lax.fori_loop(0, NC, load_case, 0)

    arrive(K_E, N8, boxes(eb))
    arrive(K_F, N8, boxes(fb))
    for i in range(AX):
        for j in range(AY):
            bx, xl, by, yl = (i + 1) // 4, (i + 1) % 4, (j + 5) // 8, (j + 5) % 8
            ex[i, j] = row(eb[bx, by, xl, yl : yl + 1, :])
            fx[i, j] = row(fb[bx, by, xl, yl : yl + 1, :])
    coefficients(
        1, lambda i, j: ex[i, j], lambda i, j: fx[i, j],
        ((0, 9), (0, 13)), ((1, 9), (1, 13)), ((1, 9), (1, 13)), co1,
    )

    arrive(K_G, N8, halo(raw, raw, 2))

    def first_rhs(i, carry):
        for c in range(3):
            for j in range(1, 13):
                k = ((c * 8 + i - 1) * 12 + j - 1) * NC
                total = fx[i, j] * (raw[c, i, j] + loadbuf[pl.ds(pl.multiple_of(k, NC), NC), :])
                total = jnp.where(ex[i, j] > 0.0, total, 0.0)
                g[0, c, i, j] = total
        return carry

    lax.fori_loop(1, 9, first_rhs, 0)

    def unpack(p):
        return jnp.where(even, p, down(p, 1)), jnp.where(even, up(p, 1), p)

    def unpack_field(packed, out, add=None):
        for c in range(3):
            for bx in range(3):
                for j in range(8):
                    for a, val in enumerate(unpack(packed[c, bx, j])):
                        i = 2 * bx + a
                        val = jnp.where(ad2[0, i, j] > 0.0, val, 0.0)
                        if add is not None:
                            val = val + add[c, i // 2 + 1, j // 2 + 1]
                        out[c, i, j] = val

    def pack_field(field, base, packed):
        for c in range(3):
            for j in range(4):
                packed[c, 1, 2 + j] = jnp.where(even, field[c, base[0], base[1] + j], field[c, base[0] + 1, base[1] + j])

    def cycle(it, carry):
        rhs = g.at[it]
        own = ((H, H + NX), (H, H + NY))
        one_out = ((H - 1, H + NX + 1), (H - 1, H + NY + 1))
        two_out = ((H - 2, H + NX + 2), (H - 2, H + NY + 2))
        x_refs = halo(a2, xb.at[it], 3)
        g2, x2, ec, g3 = g2r.at[it], x2r.at[it], ecr.at[it], g3r.at[it]

        @pl.when(it == 1)
        def _():
            def clean(i, c2_):
                for c in range(3):
                    for j in range(1, 13):
                        rhs[c, i, j] = jnp.where(ex[i, j] > 0.0, rhs[c, i, j], 0.0)
                return c2_
            lax.fori_loop(1, 9, clean, 0)

        def first(i, c2_):
            for c in range(3):
                for j in range(1, 13):
                    a1[c, i, j] = ad[c, i, j] * rhs[c, i, j]
            return c2_

        lax.fori_loop(1, 9, first, 0)
        smooth(a1, 1, *one_out, co1, w, rhs, bd, a2)
        restrict(a2, 1, *own, co1, w, rhs, t2)
        pack_field(t2, (0, 0), g2)
        start(K_G2 + it, N8, coarse_refs(g2))
        start(K_X2 + it, N8, x_refs)

        @pl.when(it == 0)
        def _():
            arrive(K_E2, N14, e2_refs)
            for i in range(10):
                for j in range(12):
                    k = (j % 4) * 2 + i % 2
                    e2x[i, j] = row(e2b[i // 2, j // 4, k : k + 1, :])
            for i in range(5):
                for j in range(6):
                    t = e2x[2 * i, 2 * j] + e2x[2 * i + 1, 2 * j] + e2x[2 * i, 2 * j + 1] + e2x[2 * i + 1, 2 * j + 1]
                    e3x[i, j] = 0.25 * pair_sum(t, 2)
            one[...] = jnp.ones((NC, NZ), F32)
            coefficients(
                2, lambda i, j: e2x[i + 2, j + 2], lambda i, j: one[...],
                ((0, 5), (0, 7)), ((1, 5), (1, 7)), ((0, 6), (0, 8)), co2,
            )
            coefficients(
                4, lambda i, j: e3x[i, j], lambda i, j: one[...],
                ((0, 4), (0, 5)), ((1, 4), (1, 5)), ((1, 4), (1, 5)), co3,
            )

        arrive(K_G2 + it, N8, coarse_refs(g2))
        unpack_field(g2, g2u)
        for c in range(3):
            for i in range(6):
                for j in range(8):
                    b1[c, i, j] = ad2[c, i, j] * g2u[c, i, j]
        own2, out2 = ((2, 4), (2, 6)), ((1, 5), (1, 7))
        smooth(b1, 2, *out2, co2, w2, g2u, bd2, b2)
        pack_field(b2, (2, 2), x2)
        start(K_X2C + it, N8, coarse_refs(x2))
        restrict(b2, 2, *own2, co2, w2, g2u, t3)
        for c in range(3):
            r0, r1 = t3[c, 0, 0], t3[c, 0, 1]
            s0, s1 = ad3[c, 2, 2] * r0, ad3[c, 2, 3] * r1
            g3[c, 2, 1] = jnp.where(low2, jnp.where(even, r0, r1), jnp.where(even, s0, s1))
        start(K_G3 + it, N14, g3_refs(g3))
        arrive(K_G3 + it, N14, g3_refs(g3))
        for c in range(3):
            for bx in range(5):
                for by in range(3):
                    for a, q in enumerate(unpack(g3[c, bx, by])):
                        keep = e3x[bx, 2 * by + a] > 0.0
                        g3u[c, bx, 2 * by + a] = jnp.where(keep, jnp.where(low2, q, down(q, 2)), 0.0)
                        c1[c, bx, 2 * by + a] = jnp.where(keep, jnp.where(low2, up(q, 2), q), 0.0)
        smooth(c1, 4, (1, 4), (1, 5), co3, w3, g3u, bd3, c2)
        arrive(K_X2C + it, N8, coarse_refs(x2))
        unpack_field(x2, b3, add=c2)
        smooth(b3, 2, *out2, co2, w2, g2u, bd2, b4)
        smooth(b4, 2, *own2, co2, w2, g2u, ad2, b1)
        pack_field(b1, (2, 2), ec)
        start(K_EC + it, N8, coarse_refs(ec))
        arrive(K_EC + it, N8, coarse_refs(ec))
        unpack_field(ec, e2u)
        arrive(K_X2 + it, N8, x_refs)

        def correct(i, rows, from_own):
            for c in range(3):
                for j in range(AY):
                    inner = from_own and H <= j < H + NY
                    old = a2[c, i, j] if inner else xb[it, c, i, j]
                    keep = ex[i, j] > 0.0
                    e = e2u[c, (i + 1) // 2, (j + 1) // 2]
                    a3[c, i, j] = jnp.where(keep, old + fx[i, j] * e, 0.0)

        for i in range(AX):
            correct(i, None, H <= i < H + NX)
        smooth(a3, 1, *two_out, co1, w, rhs, bd, a4)
        smooth(a4, 1, *one_out, co1, w, rhs, ad, pv.at[it])

        def keep_image(c, i, j, vc, av):
            g[it + 1, c, i, j] = av

        apply(pv.at[it], 1, *own, co1, w, keep_image)

        q_refs = halo(g.at[1], g.at[1], 2)

        @pl.when(it == 0)
        def _():
            start(K_G + 1, N8, q_refs)

        def gram_plane(i, accs):
            accs = list(accs)
            for c in range(3):
                for j in range(H, H + NY):
                    left = [g[q, c, i, j] for q in range(2)] + [jnp.where(it == 1, g[2, c, i, j], 0.0)]
                    for k in range(NC):
                        right = row(pv[it, c, i, j, k : k + 1, :])
                        for q in range(3):
                            accs[q * NC + k] = accs[q * NC + k] + left[q] * right
            return tuple(accs)

        zeros = tuple(jnp.zeros((NC, NZ), F32) for _ in range(3 * NC))
        accs = lax.fori_loop(H, H + NX, gram_plane, zeros)
        out = jnp.zeros((NC, NZ), F32)
        for q in range(3):
            for k in range(NC):
                out = jnp.where(lanes() == q * NC + k, row(jnp.sum(accs[q * NC + k], axis=1, keepdims=True)), out)
        gram[it] = out

        @pl.when(it == 0)
        def _():
            arrive(K_G + 1, N8, q_refs)
            sent(K_G + 1, N8, q_refs)

        sent(K_X2 + it, N8, x_refs)
        sent(K_G2 + it, N8, coarse_refs(g2))
        sent(K_X2C + it, N8, coarse_refs(x2))
        sent(K_G3 + it, N14, g3_refs(g3))
        sent(K_EC + it, N8, coarse_refs(ec))
        return carry

    lax.fori_loop(0, 2, cycle, 0)
    sent(K_E, N8, boxes(eb))
    sent(K_F, N8, boxes(fb))
    sent(K_G, N8, halo(raw, raw, 2))
    sent(K_E2, N14, e2_refs)

    def total(buffer, me, count, place, base):
        def copy(d):
            return pltpu.make_async_remote_copy(
                src_ref=buffer.at[me], dst_ref=buffer.at[me],
                send_sem=psend.at[base + d], recv_sem=precv.at[base + me],
                device_id=place(lax.rem(me + d, count)), device_id_type=MESH,
            )

        def landing(d):
            other = lax.rem(me + d, count)
            return pltpu.make_async_remote_copy(
                src_ref=buffer.at[other], dst_ref=buffer.at[other],
                send_sem=psend.at[base + d], recv_sem=precv.at[base + other],
                device_id=place(other), device_id_type=MESH,
            )

        def go(d, carry):
            copy(d).start()
            return carry

        def take(d, carry):
            landing(d).wait_recv()
            return carry

        def done(d, carry):
            copy(d).wait_send()
            return carry

        lax.fori_loop(1, count, go, 0)
        lax.fori_loop(1, count, take, 0)
        lax.fori_loop(1, count, done, 0)
        out = buffer[0]
        for k in range(1, count):
            out = out + buffer[k]
        return out

    ps1[gy] = jnp.where(lanes() < 2 * NC, gram[0], pltpu.roll(gram[1], 2 * NC, 1))
    ps2[gx] = total(ps1, gy, size_y, lambda k: (gx, k), 0)
    sums = total(ps2, gx, size_x, lambda k: (k, gy), size_y)

    rz = sums
    qp = up(sums, NC)
    ru = up(sums, 2 * NC)
    qu = up(sums, 3 * NC)
    wu = up(sums, 4 * NC)
    eye = jnp.where(lanes() == subl(), 1.0, 0.0)
    alpha = solve(qp, rz)
    inverse = solve(rz, eye)
    rz2 = rz - mm(ru, alpha) + mtm(alpha, mm(qu, alpha) - qp)
    mix = eye + mm(inverse, rz2)
    quw = mm(qu, alpha)
    pq2 = mtm(mix, mtm(qp, mix) - quw) + mtm(alpha, mtm(wu, alpha) - mtm(qu, mix))
    alpha2 = solve(pq2, rz2)
    one_m = alpha + mm(mix, alpha2)
    two_m = mm(alpha, alpha2)
    for k in range(NC):
        mats[0, k] = column(one_m, k)
        mats[1, k] = column(two_m, k)

    def finish(x, carry):
        m1 = [mats[0, k] for k in range(NC)]
        m2 = [mats[1, k] for k in range(NC)]
        i = H + x
        for c in range(3):
            for y in range(NY):
                j = H + y
                sol = jnp.zeros((NC, NZ), F32)
                res = g[0, c, i, j]
                for k in range(NC):
                    sol = sol + row(pv[0, c, i, j, k : k + 1, :]) * m1[k]
                    sol = sol - row(pv[1, c, i, j, k : k + 1, :]) * m2[k]
                    res = res - row(g[1, c, i, j, k : k + 1, :]) * m1[k]
                    res = res + row(g[2, c, i, j, k : k + 1, :]) * m2[k]
                at = pl.ds((c * NC * NX + x) * NY + y, NC, stride=NX * NY)
                xo[at, :] = sol
                ro[at, :] = res
        return carry

    lax.fori_loop(0, NX, finish, 0)


def on_device(size_x, size_y, source_field, density_class, fixed_mask, load_nodes, load_forces):
    rows = 3 * NC * NX * NY
    tile = (NC, NZ)

    def vm(*dims):
        return pltpu.VMEM(dims + tile, F32)

    def level(nx, ny):
        return [vm(nx, ny)] * 5 + [vm(3, nx, ny), vm(nx, ny), vm(nx, ny), vm(3, nx, ny), vm(3, nx, ny)]

    scratch = [
        pltpu.VMEM((3, 3, NX, NY, NZ), F32), pltpu.VMEM((3, 3, NX, NY, NZ), F32), vm(5, 3),
        vm(AX, AY), vm(AX, AY), vm(10, 12), vm(5, 6), vm(),
        vm(3, 3, AX, AY), vm(2, 3, AX, AY), vm(3, AX, AY), vm(3, AX, AY), vm(3, AX, AY), vm(3, AX, AY),
        vm(2, 3, AX, AY), vm(AX, AY), pltpu.VMEM((3 * 8 * 12 * NC, NZ), F32),
    ]
    scratch += level(AX, AY) + level(6, 8) + level(5, 6)
    scratch += [vm(3, 2, 4), vm(2, 3, 3, 8), vm(2, 3, 3, 8), vm(2, 3, 3, 8)]
    scratch += [vm(3, 6, 8)] * 5 + [vm(6, 8), vm(3, 6, 8)]
    scratch += [vm(3, 1, 2), vm(2, 3, 5, 3), vm(3, 5, 6), vm(3, 5, 6), vm(3, 5, 6), vm(5, 6)]
    scratch += [vm(2), vm(size_y), vm(size_x), vm(2, NC), vm(3, AX, AY)]
    sems = pltpu.SemaphoreType.DMA
    scratch += [sems((KINDS, len(N14))), sems((KINDS, len(N14))), sems((size_x + size_y,)), sems((size_x + size_y,))]
    spec = pl.BlockSpec(memory_space=pltpu.VMEM)
    shape = jax.ShapeDtypeStruct((rows, NZ), F32)
    sol, res = pl.pallas_call(
        functools.partial(kernel, size_x, size_y),
        out_shape=(shape, shape),
        in_specs=[spec] * 5,
        out_specs=(spec, spec),
        scratch_shapes=scratch,
        compiler_params=pltpu.CompilerParams(
            collective_id=0, has_side_effects=True, vmem_limit_bytes=56 * 1024 * 1024
        ),
        name="block_pcg",
    )(source_field.reshape(rows, NZ), density_class, fixed_mask, load_nodes, load_forces)
    return sol.reshape(source_field.shape), res.reshape(source_field.shape)


def solution(mesh):
    placed = (P(None, None, "gx", "gy", None), P("gx", "gy", None), P("gx", "gy", None), P(), P())
    return jax.shard_map(
        functools.partial(on_device, mesh.shape["gx"], mesh.shape["gy"]),
        mesh=mesh,
        in_specs=placed,
        out_specs=(P(None, None, "gx", "gy", None), P(None, None, "gx", "gy", None)),
        check_vma=False,
    )
```

```python
import functools
import math

import jax
import jax.numpy as jnp
from jax import lax
from jax.experimental import pallas as pl
from jax.experimental.pallas import tpu as pltpu
from jax.sharding import PartitionSpec as P

CLASSES = 16
MU = 1.0 / 2.6
LAM = 0.3 / 0.52
MIN_MODULUS = 0.05
STEP_A = 1.0 / (2.7 + 2.1 * math.cos(math.pi / 4.0))
STEP_B = 1.0 / (2.7 - 2.1 * math.cos(math.pi / 4.0))
MESH = pl.DeviceIdType.MESH
F32 = jnp.float32

NX, NY, NC, NZ, LOADS = 4, 8, 8, 128, 64
H = 3
AX, AY = NX + 2 * H, NY + 2 * H
N8 = [(1, 0), (-1, 0), (0, 1), (0, -1), (1, 1), (1, -1), (-1, 1), (-1, -1)]
N14 = [(dx, dy) for dx in (1, -1, 2, -2, 0) for dy in (0, 1, -1) if (dx, dy) != (0, 0)]

K_E, K_F, K_E2, K_G, K_X2, K_G2, K_X2C, K_G3, K_EC = 0, 1, 2, 3, 5, 7, 9, 11, 13
KINDS = 15


def lanes():
    return lax.broadcasted_iota(jnp.int32, (NC, NZ), 1)


def subl():
    return lax.broadcasted_iota(jnp.int32, (NC, NZ), 0)


def up(v, s):
    return pltpu.roll(v, NZ - s, 1)


def down(v, s):
    return pltpu.roll(v, s, 1)


def pair_sum(v, s):
    other = jnp.where((lanes() & s) == 0, up(v, s), down(v, s))
    return v + other


def row(v):
    return jnp.broadcast_to(v, (NC, NZ))


def span(d, n, h, base):
    if d > 0:
        return n - h, base - h, h
    if d < 0:
        return 0, base + n, h
    return 0, base, n


def coefficients(s, e_at, f_at, low, inv, co, unroll=False):
    kx, ky, kzp, kzm, dm, cw, cf, ff, ad, bd = co
    last = lanes() >= NZ - s
    first = lanes() < s
    half = 0.5 * MU

    def lower(i, carry):
        pending = []
        for j in range(*low[1]):
            e, f = e_at(i, j), f_at(i, j)
            fx, fy = f_at(i + 1, j), f_at(i, j + 1)
            fzp = jnp.where(last, 0.0, up(f, s))
            fzm = jnp.where(first, 0.0, down(f, s))
            ezp, ezm = up(e, s), down(e, s)
            le = LAM * e
            hf = half * f
            pending += [
                (kx, (i, j), (e + e_at(i + 1, j)) * (hf * fx)),
                (ky, (i, j), (e + e_at(i, j + 1)) * (hf * fy)),
                (kzp, (i, j), (e + ezp) * (hf * fzp)),
                (kzm, (i, j), (ezm + e) * (hf * fzm)),
                (cw, (0, i, j), le * fx),
                (cw, (1, i, j), le * fy),
                (cw, (2, i, j), le * fzp),
                (cf, (i, j), le * f),
                (ff, (i, j), f),
            ]
            if j % 3 == 2 or j == low[1][1] - 1:
                for ref, idx, val in pending:
                    ref[idx] = val
                pending = []
        return carry

    loop(low[0][0], low[0][1], lower, unroll)

    def smoother(i, carry):
        pending = []
        for j in range(*inv[1]):
            e, f = e_at(i, j), f_at(i, j)
            ezp = jnp.where(last, 0.0, up(e, s))
            ezm = jnp.where(first, 0.0, down(e, s))
            ex, ey = e_at(i - 1, j), e_at(i, j - 1)
            d = half * (ex + e_at(i + 1, j) + ey + e_at(i, j + 1) + ezm + ezp + 6.0 * e)
            pending.append((dm, (i, j), f * d + (1.0 - f)))
            for c, below in enumerate((ex, ey, ezm)):
                diag = jnp.where(e > 0.0, d + LAM * (e + below), 1.0)
                dinv = jnp.where(e > 0.0, f / diag + (1.0 - f), 0.0)
                pending.append((ad, (c, i, j), STEP_A * dinv))
                pending.append((bd, (c, i, j), STEP_B * dinv))
            if j % 3 == 2 or j == inv[1][1] - 1:
                for ref, idx, val in pending:
                    ref[idx] = val
                pending = []
        return carry

    loop(inv[0][0], inv[0][1], smoother, unroll)


def sweep(v, s, xr, yr, co, w, emit, chunk, unroll):
    kx, ky, kzp, kzm, dm, cw, cf, ff = co[:8]
    wmask = lanes() < s

    def spread(i, j, centre, ahead_x, ahead_y, ahead_z):
        total = centre[0] + centre[1] + centre[2]
        return cw[0, i, j] * ahead_x + cw[1, i, j] * ahead_y + cw[2, i, j] * ahead_z - cf[i, j] * total

    def at(i, j):
        return [v[c, i, j] for c in range(3)]

    before = xr[0] - 1
    stores = []
    for j in range(*yr):
        centre = at(before, j)
        stores.append((j, spread(before, j, centre, v[0, before + 1, j], v[1, before, j + 1], up(centre[2], s))))
    for j, val in stores:
        w[before, j] = val

    def body(i, carry):
        j0 = yr[0] - 1
        prev = at(i, j0)
        here = at(i, yr[0])
        wprev = spread(i, j0, prev, v[0, i + 1, j0], here[1], up(prev[2], s))
        kyprev = ky[i, j0]
        for ja in range(yr[0], yr[1], chunk):
            rows, ws = {}, []
            for j in range(ja, min(ja + chunk, yr[1])):
                nxt = at(i, j + 1)
                ahead = [v[c, i + 1, j] for c in range(3)]
                zp = [up(here[c], s) for c in range(3)]
                zm = [down(here[c], s) for c in range(3)]
                wc = spread(i, j, here, ahead[0], nxt[1], zp[2])
                below = (w[i - 1, j], wprev, jnp.where(wmask, 0.0, down(wc, s)))
                k = (kx[i, j], kx[i - 1, j], ky[i, j], kyprev, kzp[i, j], kzm[i, j])
                f, d = ff[i, j], dm[i, j]
                out = []
                for c in range(3):
                    one = d * here[c] + f * (below[c] - wc)
                    two = k[0] * ahead[c] + k[1] * v[c, i - 1, j]
                    three = k[2] * nxt[c] + k[3] * prev[c]
                    four = k[4] * zp[c] + k[5] * zm[c]
                    out.append((here[c], (one - two) - (three + four)))
                rows[j] = out
                ws.append((j, wc))
                prev, here, wprev, kyprev = here, nxt, wc, k[2]
            pending = emit(i, rows)
            for j, val in ws:
                w[i, j] = val
            for ref, idx, val in pending:
                ref[idx] = val
        return carry

    loop(xr[0], xr[1], body, unroll)


def loop(lo, hi, body, unroll):
    if unroll:
        for i in range(lo, hi):
            body(i, 0)
    else:
        lax.fori_loop(lo, hi, body, 0)


def smooth(v, s, xr, yr, co, w, rhs, step, out, chunk=4, unroll=False):
    def emit(i, rows):
        return [
            (out, (c, i, j), vc + step[c, i, j] * (rhs[c, i, j] - av))
            for j, vals in rows.items()
            for c, (vc, av) in enumerate(vals)
        ]

    sweep(v, s, xr, yr, co, w, emit, chunk, unroll)


def restrict(v, s, xr, yr, co, w, rhs, part, coarse, unroll=False):
    def emit(i, rows):
        pending = []
        for j in list(rows)[::2]:
            for c in range(3):
                total = (rhs[c, i, j] - rows[j][c][1]) + (rhs[c, i, j + 1] - rows[j + 1][c][1])
                pending.append((part, (c, i - xr[0], (j - yr[0]) // 2), total))
        return pending

    sweep(v, s, xr, yr, co, w, emit, 4, unroll)
    pending = []
    for c in range(3):
        for q in range((xr[1] - xr[0]) // 2):
            for y2 in range((yr[1] - yr[0]) // 2):
                pending.append(((c, q, y2), pair_sum(part[c, 2 * q, y2] + part[c, 2 * q + 1, y2], s)))
    for idx, val in pending:
        coarse[idx] = val


def column(m, i):
    picked = jnp.where(lanes() == subl(), row(m[i : i + 1, :]), 0.0)
    return row(jnp.sum(picked, axis=1, keepdims=True))


def tree(terms):
    while len(terms) > 1:
        terms = [sum(terms[k : k + 2]) for k in range(0, len(terms), 2)]
    return terms[0]


def mm(a, b):
    return sum(row(a[:, k : k + 1]) * row(b[k : k + 1, :]) for k in range(NC))


def mtm(a, b):
    return sum(column(a, k) * row(b[k : k + 1, :]) for k in range(NC))


def solve(matrix, rhs):
    aug = jnp.where(lanes() < NC, matrix, pltpu.roll(rhs, NC, 1))
    for k in range(NC):
        scaled = row(aug[k : k + 1, :]) / row(aug[k : k + 1, k : k + 1])
        aug = jnp.where(subl() == k, scaled, aug - row(aug[:, k : k + 1]) * scaled)
    return up(aug, NC)


def kernel(
    size_x, size_y,
    src, dens, mask, nodes, forces, xo, ro,
    eb, fb, e2b, ex, fx, e2x, e3x, one,
    g, pv, a1, a2, a3, a4, xb, w, loadbuf,
    kx, ky, kzp, kzm, dm, cw, cf, ff, ad, bd,
    kx2, ky2, kzp2, kzm2, dm2, cw2, cf2, ff2, ad2, bd2,
    kx3, ky3, kzp3, kzm3, dm3, cw3, cf3, ff3, ad3, bd3,
    t2, g2r, x2r, ecr, g2u, b1, b2, b3, b4, w2, e2u,
    t3, g3r, g3u, c1, c2, w3,
    gram, ps1, ps2, mats, raw, part,
    send, recv, psend, precv,
):
    gx, gy = lax.axis_index("gx"), lax.axis_index("gy")
    co1 = (kx, ky, kzp, kzm, dm, cw, cf, ff, ad, bd)
    co2 = (kx2, ky2, kzp2, kzm2, dm2, cw2, cf2, ff2, ad2, bd2)
    co3 = (kx3, ky3, kzp3, kzm3, dm3, cw3, cf3, ff3, ad3, bd3)
    even = (lanes() & 1) == 0
    low2 = (lanes() & 2) == 0

    def valid(dx, dy):
        return (gx + dx >= 0) & (gx + dx < size_x) & (gy + dy >= 0) & (gy + dy < size_y)

    def message(kind, k, d, refs):
        a, b = refs(*d)
        return pltpu.make_async_remote_copy(
            src_ref=a, dst_ref=b, send_sem=send.at[kind, k], recv_sem=recv.at[kind, k],
            device_id=(gx + d[0], gy + d[1]), device_id_type=MESH,
        )

    def start(kind, group, refs):
        for k, d in enumerate(group):
            @pl.when(valid(*d))
            def _():
                message(kind, k, d, refs).start()

    def arrive(kind, group, refs):
        for k, d in enumerate(group):
            @pl.when(valid(-d[0], -d[1]))
            def _():
                message(kind, k, d, refs).wait_recv()

    def sent(kind, group, refs):
        for k, d in enumerate(group):
            @pl.when(valid(*d))
            def _():
                message(kind, k, d, refs).wait_send()

    def boxes(ref):
        return lambda dx, dy: (ref.at[1, 1], ref.at[1 - dx, 1 - dy])

    def e2_refs(dx, dy):
        return e2b.at[2, 1], e2b.at[2 - dx, 1 - dy]

    def halo(source, target, h, skip=0):
        def side(d, other, n):
            if d == 0:
                return 0, H, n
            near, far = (skip, h) if other == 0 else (0, h - 1 if other == d else h)
            return (n - far, H - far, far - near) if d > 0 else (near, H + n + near, far - near)

        def refs(dx, dy):
            sx, tx, nx = side(dx, dy, NX)
            sy, ty, ny = side(dy, dx, NY)
            a = source.at[:, pl.ds(H + sx, nx), pl.ds(H + sy, ny)]
            return a, target.at[:, pl.ds(tx, nx), pl.ds(ty, ny)]
        return refs

    def coarse_refs(ref):
        def refs(dx, dy):
            sy, ty, ny = span(dy, 4, 2, 2)
            return ref.at[:, 1, pl.ds(2 + sy, ny)], ref.at[:, 1 - dx, pl.ds(ty, ny)]
        return refs

    def g3_refs(ref):
        return lambda dx, dy: (ref.at[:, 2, 1], ref.at[:, 2 - dx, 1 - dy])

    zero3 = jnp.zeros((NX, NY, NZ), F32)
    for bx in range(3):
        for by in range(3):
            eb[bx, by] = zero3
            fb[bx, by] = zero3
    for bx in range(5):
        for by in range(3):
            e2b[bx, by] = jnp.zeros((NC, NZ), F32)
    for x in range(NX):
        rel = (dens[x].astype(F32) + 1.0) / CLASSES
        eb[1, 1, x] = MIN_MODULUS + (1.0 - MIN_MODULUS) * rel * rel * rel
        fb[1, 1, x] = 1.0 - mask[x].astype(F32)
    halves = []
    for q in range(2):
        t = eb[1, 1, 2 * q] + eb[1, 1, 2 * q + 1]
        halves.append(0.25 * pair_sum(t + pltpu.roll(t, NY - 1, 0), 1))
    e2b[2, 1] = jnp.where((subl() & 1) == 0, halves[0], pltpu.roll(halves[1], 1, 0))

    for c in range(3):
        for x in range(NX):
            for y in range(NY):
                raw[c, H + x, H + y] = src[pl.ds((c * NC * NX + x) * NY + y, NC, stride=NX * NY), :]

    bar = pltpu.get_barrier_semaphore()
    corners = [(dx, dy) for dx in (1, -1, 2, -2) for dy in (1, -1)]
    peers = jnp.int32(size_x + size_y - 2)

    for d in range(1, size_x):
        pl.semaphore_signal(bar, inc=1, device_id=(lax.rem(gx + d, size_x), gy), device_id_type=MESH)
    for d in range(1, size_y):
        pl.semaphore_signal(bar, inc=1, device_id=(gx, lax.rem(gy + d, size_y)), device_id_type=MESH)
    for d in corners:
        peers = peers + jnp.where(valid(*d), 1, 0)

        @pl.when(valid(*d))
        def _():
            pl.semaphore_signal(bar, inc=1, device_id=(gx + d[0], gy + d[1]), device_id_type=MESH)
    pl.semaphore_wait(bar, peers)

    start(K_E, N8, boxes(eb))
    start(K_F, N8, boxes(fb))
    start(K_G, N8, halo(raw, raw, 2))
    start(K_E2, N14, e2_refs)

    def load_case(i, carry):
        node = nodes[pl.ds(i, 1), :]
        nz = lax.rem(node, NZ)
        nyx = lax.div(node, NZ)
        ny = lax.rem(nyx, size_y * NY) - gy * NY + 2
        nx = lax.div(nyx, size_y * NY) - gx * NX + 2
        hot = jnp.where(lax.broadcasted_iota(jnp.int32, (NZ, LOADS), 0) == nz, 1.0, 0.0)
        rows = lax.broadcasted_iota(jnp.int32, (16, LOADS), 0)
        parts = []
        for c in range(3):
            force = forces[c, pl.ds(i, 1), :]
            for x in range(8):
                parts.append(jnp.where((rows == ny) & (nx == x), force, 0.0))
        got = lax.dot_general(
            jnp.concatenate(parts, axis=0), hot, (((1,), (1,)), ((), ())),
            precision=lax.Precision.HIGHEST, preferred_element_type=F32,
        )
        for k in range(24):
            loadbuf[pl.ds(k * 96 + i, 8, stride=NC), :] = got[16 * k : 16 * k + 8]
            loadbuf[pl.ds(k * 96 + 64 + i, 4, stride=NC), :] = got[16 * k + 8 : 16 * k + 12]
        return carry

    lax.fori_loop(0, NC, load_case, 0)

    arrive(K_E, N8, boxes(eb))
    arrive(K_F, N8, boxes(fb))
    for i in range(AX):
        for j in range(AY):
            bx, xl, by, yl = (i + 1) // 4, (i + 1) % 4, (j + 5) // 8, (j + 5) % 8
            ex[i, j] = row(eb[bx, by, xl, yl : yl + 1, :])
            fx[i, j] = row(fb[bx, by, xl, yl : yl + 1, :])
    coefficients(
        1, lambda i, j: ex[i, j], lambda i, j: fx[i, j],
        ((0, 9), (0, 13)), ((1, 9), (1, 13)), co1,
    )

    arrive(K_G, N8, halo(raw, raw, 2))

    def first_rhs(i, carry):
        for c in range(3):
            pending = []
            for j in range(1, 13):
                k = ((c * 8 + i - 1) * 12 + j - 1) * NC
                total = fx[i, j] * (raw[c, i, j] + loadbuf[pl.ds(pl.multiple_of(k, NC), NC), :])
                pending.append((j, jnp.where(ex[i, j] > 0.0, total, 0.0)))
            for j, val in pending:
                g[0, c, i, j] = val
        return carry

    lax.fori_loop(1, 9, first_rhs, 0)

    def unpack(p):
        return jnp.where(even, p, down(p, 1)), jnp.where(even, up(p, 1), p)

    def unpack_field(packed, out, add=None):
        for c in range(3):
            for bx in range(3):
                pending = []
                for j in range(8):
                    for a, val in enumerate(unpack(packed[c, bx, j])):
                        i = 2 * bx + a
                        val = jnp.where(ad2[0, i, j] > 0.0, val, 0.0)
                        if add is not None:
                            val = val + add[c, i // 2 + 1, j // 2 + 1]
                        pending.append(((c, i, j), val))
                for idx, val in pending:
                    out[idx] = val

    def pack_field(field, base, packed):
        for c in range(3):
            for j in range(4):
                packed[c, 1, 2 + j] = jnp.where(even, field[c, base[0], base[1] + j], field[c, base[0] + 1, base[1] + j])

    def cycle(it, carry):
        rhs = g.at[it]
        own = ((H, H + NX), (H, H + NY))
        one_out = ((H - 1, H + NX + 1), (H - 1, H + NY + 1))
        two_out = ((H - 2, H + NX + 2), (H - 2, H + NY + 2))
        x_refs = halo(a2, xb.at[it], 3, 1)
        g2, x2, ec, g3 = g2r.at[it], x2r.at[it], ecr.at[it], g3r.at[it]

        @pl.when(it == 1)
        def _():
            def clean(i, c2_):
                for c in range(3):
                    pending = [(j, jnp.where(ex[i, j] > 0.0, rhs[c, i, j], 0.0)) for j in range(1, 13)]
                    for j, val in pending:
                        rhs[c, i, j] = val
                return c2_
            lax.fori_loop(1, 9, clean, 0)

        def first(i, c2_):
            for c in range(3):
                pending = [(j, ad[c, i, j] * rhs[c, i, j]) for j in range(1, 13)]
                for j, val in pending:
                    a1[c, i, j] = val
            return c2_

        lax.fori_loop(1, 9, first, 0)
        smooth(a1, 1, *one_out, co1, w, rhs, bd, a2, 5)
        restrict(a2, 1, *own, co1, w, rhs, part, t2)
        pack_field(t2, (0, 0), g2)
        start(K_G2 + it, N8, coarse_refs(g2))

        @pl.when(it == 0)
        def _():
            arrive(K_E2, N14, e2_refs)
            for i in range(10):
                for j in range(12):
                    k = (j % 4) * 2 + i % 2
                    e2x[i, j] = row(e2b[i // 2, j // 4, k : k + 1, :])
            for i in range(5):
                for j in range(6):
                    t = e2x[2 * i, 2 * j] + e2x[2 * i + 1, 2 * j] + e2x[2 * i, 2 * j + 1] + e2x[2 * i + 1, 2 * j + 1]
                    e3x[i, j] = 0.25 * pair_sum(t, 2)
            one[...] = jnp.ones((NC, NZ), F32)
            coefficients(
                2, lambda i, j: e2x[i + 2, j + 2], lambda i, j: one[...],
                ((0, 5), (0, 7)), ((0, 6), (0, 8)), co2,
            )
            coefficients(
                4, lambda i, j: e3x[i, j], lambda i, j: one[...],
                ((0, 4), (0, 5)), ((1, 4), (1, 5)), co3,
            )

        arrive(K_G2 + it, N8, coarse_refs(g2))
        unpack_field(g2, g2u)
        for c in range(3):
            for i in range(6):
                for j in range(8):
                    b1[c, i, j] = ad2[c, i, j] * g2u[c, i, j]
        own2, out2 = ((2, 4), (2, 6)), ((1, 5), (1, 7))
        smooth(b1, 2, *out2, co2, w2, g2u, bd2, b2, 3)
        pack_field(b2, (2, 2), x2)
        start(K_X2C + it, N8, coarse_refs(x2))
        restrict(b2, 2, *own2, co2, w2, g2u, part, t3)
        for c in range(3):
            r0, r1 = t3[c, 0, 0], t3[c, 0, 1]
            s0, s1 = ad3[c, 2, 2] * r0, ad3[c, 2, 3] * r1
            g3[c, 2, 1] = jnp.where(low2, jnp.where(even, r0, r1), jnp.where(even, s0, s1))
        start(K_G3 + it, N14, g3_refs(g3))
        start(K_X2 + it, N8, x_refs)
        arrive(K_G3 + it, N14, g3_refs(g3))
        for c in range(3):
            for bx in range(5):
                for by in range(3):
                    for a, q in enumerate(unpack(g3[c, bx, by])):
                        keep = e3x[bx, 2 * by + a] > 0.0
                        g3u[c, bx, 2 * by + a] = jnp.where(keep, jnp.where(low2, q, down(q, 2)), 0.0)
                        c1[c, bx, 2 * by + a] = jnp.where(keep, jnp.where(low2, up(q, 2), q), 0.0)
        smooth(c1, 4, (1, 4), (1, 5), co3, w3, g3u, bd3, c2, 4)
        arrive(K_X2C + it, N8, coarse_refs(x2))
        unpack_field(x2, b3, add=c2)
        smooth(b3, 2, *out2, co2, w2, g2u, bd2, b4, 3)
        smooth(b4, 2, *own2, co2, w2, g2u, ad2, b1, 4)
        pack_field(b1, (2, 2), ec)
        start(K_EC + it, N8, coarse_refs(ec))
        arrive(K_EC + it, N8, coarse_refs(ec))
        unpack_field(ec, e2u)
        arrive(K_X2 + it, N8, x_refs)

        def correct(i, from_own):
            for c in range(3):
                pending = []
                for j in range(AY):
                    inner = from_own(j)
                    old = a2[c, i, j] if inner else xb[it, c, i, j]
                    keep = ex[i, j] > 0.0
                    e = e2u[c, (i + 1) // 2, (j + 1) // 2]
                    pending.append((j, jnp.where(keep, old + fx[i, j] * e, 0.0)))
                for j, val in pending:
                    a3[c, i, j] = val

        for i in range(AX):
            out = 0 if H <= i < H + NX else 1 if H - 1 <= i <= H + NX else 9
            correct(i, lambda j: out + (not H <= j < H + NY) + 9 * (not H - 1 <= j <= H + NY) < 2)
        smooth(a3, 1, *two_out, co1, w, rhs, bd, a4)
        smooth(a4, 1, *one_out, co1, w, rhs, ad, pv.at[it], 5)

        def keep_image(i, rows):
            return [(g, (it + 1, c, i, j), av) for j, vals in rows.items() for c, (_, av) in enumerate(vals)]

        sweep(pv.at[it], 1, *own, co1, w, keep_image, 4, False)

        q_refs = halo(g.at[1], g.at[1], 2)

        @pl.when(it == 0)
        def _():
            start(K_G + 1, N8, q_refs)

        def gram_plane(i, accs):
            accs = list(accs)
            for c in range(3):
                for j in range(H, H + NY):
                    left = [g[q, c, i, j] for q in range(2)] + [jnp.where(it == 1, g[2, c, i, j], 0.0)]
                    for k in range(NC):
                        right = row(pv[it, c, i, j, k : k + 1, :])
                        for q in range(3):
                            accs[q * NC + k] = accs[q * NC + k] + left[q] * right
            return tuple(accs)

        zeros = tuple(jnp.zeros((NC, NZ), F32) for _ in range(3 * NC))
        accs = lax.fori_loop(H, H + NX, gram_plane, zeros)
        out = jnp.zeros((NC, NZ), F32)
        for q in range(3):
            for k in range(NC):
                out = jnp.where(lanes() == q * NC + k, row(jnp.sum(accs[q * NC + k], axis=1, keepdims=True)), out)
        gram[it] = out

        @pl.when(it == 0)
        def _():
            arrive(K_G + 1, N8, q_refs)
            sent(K_G + 1, N8, q_refs)

        sent(K_X2 + it, N8, x_refs)
        sent(K_G2 + it, N8, coarse_refs(g2))
        sent(K_X2C + it, N8, coarse_refs(x2))
        sent(K_G3 + it, N14, g3_refs(g3))
        sent(K_EC + it, N8, coarse_refs(ec))
        return carry

    lax.fori_loop(0, 2, cycle, 0)
    sent(K_E, N8, boxes(eb))
    sent(K_F, N8, boxes(fb))
    sent(K_G, N8, halo(raw, raw, 2))
    sent(K_E2, N14, e2_refs)

    def total(buffer, me, count, place, base):
        def copy(d):
            return pltpu.make_async_remote_copy(
                src_ref=buffer.at[me], dst_ref=buffer.at[me],
                send_sem=psend.at[base + d], recv_sem=precv.at[base + me],
                device_id=place(lax.rem(me + d, count)), device_id_type=MESH,
            )

        def landing(d):
            other = lax.rem(me + d, count)
            return pltpu.make_async_remote_copy(
                src_ref=buffer.at[other], dst_ref=buffer.at[other],
                send_sem=psend.at[base + d], recv_sem=precv.at[base + other],
                device_id=place(other), device_id_type=MESH,
            )

        for d in range(1, count):
            copy(d).start()
        for d in range(1, count):
            landing(d).wait_recv()
        for d in range(1, count):
            copy(d).wait_send()
        out = buffer[0]
        for k in range(1, count):
            out = out + buffer[k]
        return out

    ps1[gy] = jnp.where(lanes() < 2 * NC, gram[0], pltpu.roll(gram[1], 2 * NC, 1))
    ps2[gx] = total(ps1, gy, size_y, lambda k: (gx, k), 0)
    sums = total(ps2, gx, size_x, lambda k: (k, gy), size_y)

    rz = sums
    qp = up(sums, NC)
    ru = up(sums, 2 * NC)
    qu = up(sums, 3 * NC)
    wu = up(sums, 4 * NC)
    eye = jnp.where(lanes() == subl(), 1.0, 0.0)
    alpha = solve(qp, rz)
    inverse = solve(rz, eye)
    rz2 = rz - mm(ru, alpha) + mtm(alpha, mm(qu, alpha) - qp)
    mix = eye + mm(inverse, rz2)
    quw = mm(qu, alpha)
    pq2 = mtm(mix, mtm(qp, mix) - quw) + mtm(alpha, mtm(wu, alpha) - mtm(qu, mix))
    alpha2 = solve(pq2, rz2)
    one_m = alpha + mm(mix, alpha2)
    two_m = mm(alpha, alpha2)
    for k in range(NC):
        mats[0, k] = column(one_m, k)
        mats[1, k] = column(two_m, k)

    def finish(x, carry):
        m1 = [mats[0, k] for k in range(NC)]
        m2 = [mats[1, k] for k in range(NC)]
        i = H + x
        def blend(one, two, c, j):
            terms = [row(one[c, i, j, k : k + 1, :]) * m1[k] for k in range(NC)]
            other = [row(two[c, i, j, k : k + 1, :]) * m2[k] for k in range(NC)]
            return tree(terms) - tree(other)

        for c in range(3):
            pending = []
            for y in range(NY):
                j = H + y
                at = pl.ds((c * NC * NX + x) * NY + y, NC, stride=NX * NY)
                pending.append((xo, at, blend(pv.at[0], pv.at[1], c, j)))
                pending.append((ro, at, g[0, c, i, j] - blend(g.at[1], g.at[2], c, j)))
            for ref, at, val in pending:
                ref[at, :] = val
        return carry

    lax.fori_loop(0, NX, finish, 0)


def on_device(size_x, size_y, source_field, density_class, fixed_mask, load_nodes, load_forces):
    rows = 3 * NC * NX * NY
    tile = (NC, NZ)

    def vm(*dims):
        return pltpu.VMEM(dims + tile, F32)

    def level(nx, ny):
        return [vm(nx, ny)] * 5 + [vm(3, nx, ny), vm(nx, ny), vm(nx, ny), vm(3, nx, ny), vm(3, nx, ny)]

    scratch = [
        pltpu.VMEM((3, 3, NX, NY, NZ), F32), pltpu.VMEM((3, 3, NX, NY, NZ), F32), vm(5, 3),
        vm(AX, AY), vm(AX, AY), vm(10, 12), vm(5, 6), vm(),
        vm(3, 3, AX, AY), vm(2, 3, AX, AY), vm(3, AX, AY), vm(3, AX, AY), vm(3, AX, AY), vm(3, AX, AY),
        vm(2, 3, AX, AY), vm(AX, AY), pltpu.VMEM((3 * 8 * 12 * NC, NZ), F32),
    ]
    scratch += level(AX, AY) + level(6, 8) + level(5, 6)
    scratch += [vm(3, 2, 4), vm(2, 3, 3, 8), vm(2, 3, 3, 8), vm(2, 3, 3, 8)]
    scratch += [vm(3, 6, 8)] * 5 + [vm(6, 8), vm(3, 6, 8)]
    scratch += [vm(3, 1, 2), vm(2, 3, 5, 3), vm(3, 5, 6), vm(3, 5, 6), vm(3, 5, 6), vm(5, 6)]
    scratch += [vm(2), vm(size_y), vm(size_x), vm(2, NC), vm(3, AX, AY), vm(3, NX, 4)]
    sems = pltpu.SemaphoreType.DMA
    scratch += [sems((KINDS, len(N14))), sems((KINDS, len(N14))), sems((size_x + size_y,)), sems((size_x + size_y,))]
    spec = pl.BlockSpec(memory_space=pltpu.VMEM)
    shape = jax.ShapeDtypeStruct((rows, NZ), F32)
    sol, res = pl.pallas_call(
        functools.partial(kernel, size_x, size_y),
        out_shape=(shape, shape),
        in_specs=[spec] * 5,
        out_specs=(spec, spec),
        scratch_shapes=scratch,
        compiler_params=pltpu.CompilerParams(
            collective_id=0, has_side_effects=True, vmem_limit_bytes=56 * 1024 * 1024
        ),
        name="block_pcg",
    )(source_field.reshape(rows, NZ), density_class, fixed_mask, load_nodes, load_forces)
    return sol.reshape(source_field.shape), res.reshape(source_field.shape)


def solution(mesh):
    placed = (P(None, None, "gx", "gy", None), P("gx", "gy", None), P("gx", "gy", None), P(), P())
    return jax.shard_map(
        functools.partial(on_device, mesh.shape["gx"], mesh.shape["gy"]),
        mesh=mesh,
        in_specs=placed,
        out_specs=(P(None, None, "gx", "gy", None), P(None, None, "gx", "gy", None)),
        check_vma=False,
    )
```

```python
import functools
import math

import jax
import jax.numpy as jnp
from jax import lax
from jax.experimental import pallas as pl
from jax.experimental.pallas import tpu as pltpu
from jax.sharding import PartitionSpec as P

CLASSES = 16
MU = 1.0 / 2.6
LAM = 0.3 / 0.52
MIN_MODULUS = 0.05
STEP_A = 1.0 / (2.7 + 2.1 * math.cos(math.pi / 4.0))
STEP_B = 1.0 / (2.7 - 2.1 * math.cos(math.pi / 4.0))
MESH = pl.DeviceIdType.MESH
F32 = jnp.float32

NX, NY, NC, NZ, LOADS = 4, 8, 8, 128, 64
H = 3
AX, AY = NX + 2 * H, NY + 2 * H
N8 = [(1, -1), (-1, 1), (1, 1), (-1, -1), (1, 0), (-1, 0), (0, 1), (0, -1)]
N14 = [(dx, dy) for dx in (2, -2, 1, -1, 0) for dy in (1, -1, 0) if (dx, dy) != (0, 0)]

K_E, K_F, K_E2, K_G, K_X2, K_G2, K_X2C, K_G3, K_EC = 0, 1, 2, 3, 5, 7, 9, 11, 13
KINDS = 15
PIECES = 4


def far_first(count):
    return sorted(range(1, count), key=lambda d: abs(d - count / 2))


def lanes():
    return lax.broadcasted_iota(jnp.int32, (NC, NZ), 1)


def subl():
    return lax.broadcasted_iota(jnp.int32, (NC, NZ), 0)


def up(v, s):
    return pltpu.roll(v, NZ - s, 1)


def down(v, s):
    return pltpu.roll(v, s, 1)


def pair_sum(v, s):
    other = jnp.where((lanes() & s) == 0, up(v, s), down(v, s))
    return v + other


def row(v):
    return jnp.broadcast_to(v, (NC, NZ))


def span(d, n, h, base):
    if d > 0:
        return n - h, base - h, h
    if d < 0:
        return 0, base + n, h
    return 0, base, n


def coefficients(s, e_at, f_at, low, inv, co, unroll=False):
    kx, ky, kzp, fup, dm, cw, cf, ff, ad, bd = co
    last = lanes() >= NZ - s
    first = lanes() < s
    half = 0.5 * MU

    def lower(i, carry):
        pending = []
        for j in range(*low[1]):
            e, f = e_at(i, j), f_at(i, j)
            fx, fy = f_at(i + 1, j), f_at(i, j + 1)
            fzp = jnp.where(last, 0.0, up(f, s))
            ezp = up(e, s)
            le = LAM * e
            hf = half * f
            pending += [
                (kx, (i, j), (e + e_at(i + 1, j)) * (hf * fx)),
                (ky, (i, j), (e + e_at(i, j + 1)) * (hf * fy)),
                (kzp, (i, j), (e + ezp) * (hf * fzp)),
                (fup, (i, j), fzp),
                (cw, (0, i, j), le * fx),
                (cw, (1, i, j), le * fy),
                (cw, (2, i, j), le * fzp),
                (cf, (i, j), le * f),
                (ff, (i, j), f),
            ]
            if j % 3 == 2 or j == low[1][1] - 1:
                for ref, idx, val in pending:
                    ref[idx] = val
                pending = []
        return carry

    loop(low[0][0], low[0][1], lower, unroll)

    def smoother(i, carry):
        pending = []
        for j in range(*inv[1]):
            e, f = e_at(i, j), f_at(i, j)
            ezp = jnp.where(last, 0.0, up(e, s))
            ezm = jnp.where(first, 0.0, down(e, s))
            ex, ey = e_at(i - 1, j), e_at(i, j - 1)
            d = half * (ex + e_at(i + 1, j) + ey + e_at(i, j + 1) + ezm + ezp + 6.0 * e)
            pending.append((dm, (i, j), f * d + (1.0 - f)))
            for c, below in enumerate((ex, ey, ezm)):
                diag = jnp.where(e > 0.0, d + LAM * (e + below), 1.0)
                dinv = jnp.where(e > 0.0, f / diag + (1.0 - f), 0.0)
                pending.append((ad, (c, i, j), STEP_A * dinv))
                pending.append((bd, (c, i, j), STEP_B * dinv))
            if j % 3 == 2 or j == inv[1][1] - 1:
                for ref, idx, val in pending:
                    ref[idx] = val
                pending = []
        return carry

    loop(inv[0][0], inv[0][1], smoother, unroll)


def compact_coefficients(e_ref, f_ref, co, ex, fx):
    kx, ky, kzp, fup, dm, cw, cf, ff, ad, bd = co
    half = 0.5 * MU
    wide = (16, NZ)
    lane = lax.broadcasted_iota(jnp.int32, wide, 1)

    def zup(v):
        return jnp.where(lane == NZ - 1, 0.0, pltpu.roll(v, NZ - 1, 1))

    def ynext(v):
        return pltpu.roll(v, 15, 0)

    def plane(i, carry):
        e, f, e1, f1 = e_ref[i], f_ref[i], e_ref[i + 1], f_ref[i + 1]
        fy, fz = ynext(f), zup(f)
        le, hf = LAM * e, half * f
        ahead = (
            (ex, (i,), e), (fx, (i,), f),
            (kx, (i,), (e + e1) * (hf * f1)),
            (ky, (i,), (e + ynext(e)) * (hf * fy)),
            (kzp, (i,), (e + zup(e)) * (hf * fz)),
            (fup, (i,), fz), (cw, (0, i), le * f1), (cw, (1, i), le * fy),
            (cw, (2, i), le * fz), (cf, (i,), le * f), (ff, (i,), f),
        )
        for ref, at, val in ahead:
            for j in range(AY):
                ref[at + (j,)] = row(val[j : j + 1, :])
        return carry

    lax.fori_loop(0, AX - 1, plane, 0)
    for ref, source in ((ex, e_ref), (fx, f_ref)):
        last = source[AX - 1]
        for j in range(AY):
            ref[AX - 1, j] = row(last[j : j + 1, :])

    def smoother(i, carry):
        e, f = e_ref[i], f_ref[i]
        ey = pltpu.roll(e, 1, 0)
        ez = jnp.where(lane == 0, 0.0, pltpu.roll(e, 1, 1))
        eb = e_ref[i - 1]
        d = half * (eb + e_ref[i + 1] + ey + ynext(e) + ez + zup(e) + 6.0 * e)
        out = [(dm, (i,), f * d + (1.0 - f))]
        for c, below in enumerate((eb, ey, ez)):
            diag = jnp.where(e > 0.0, d + LAM * (e + below), 1.0)
            dinv = jnp.where(e > 0.0, f / diag + (1.0 - f), 0.0)
            out += [(ad, (c, i), STEP_A * dinv), (bd, (c, i), STEP_B * dinv)]
        for ref, at, val in out:
            for j in range(1, AY - 1):
                ref[at + (j,)] = row(val[j : j + 1, :])
        return carry

    lax.fori_loop(1, AX - 1, smoother, 0)


def sweep(v, s, xr, yr, co, w, emit, chunk, unroll):
    kx, ky, kzp, fup, dm, cw, cf, ff = co[:8]

    def spread(i, j, centre, ahead_x, ahead_y, ahead_z):
        total = centre[0] + centre[1] + centre[2]
        return cw[0, i, j] * ahead_x + cw[1, i, j] * ahead_y + cw[2, i, j] * ahead_z - cf[i, j] * total

    def at(i, j):
        return [v[c, i, j] for c in range(3)]

    before = xr[0] - 1
    stores = []
    for j in range(*yr):
        centre = at(before, j)
        stores.append((j, spread(before, j, centre, v[0, before + 1, j], v[1, before, j + 1], up(centre[2], s))))
    for j, val in stores:
        w[before, j] = val

    def body(i, carry):
        j0 = yr[0] - 1
        prev = at(i, j0)
        here = at(i, yr[0])
        wprev = spread(i, j0, prev, v[0, i + 1, j0], here[1], up(prev[2], s))
        kyprev = ky[i, j0]
        for ja in range(yr[0], yr[1], chunk):
            rows, ws = {}, []
            for j in range(ja, min(ja + chunk, yr[1])):
                nxt = at(i, j + 1)
                ahead = [v[c, i + 1, j] for c in range(3)]
                zp = [up(here[c], s) for c in range(3)]
                wc = spread(i, j, here, ahead[0], nxt[1], zp[2])
                k = (kx[i, j], kx[i - 1, j], ky[i, j], kyprev, kzp[i, j])
                f, d = ff[i, j], dm[i, j]
                fwc = f * wc
                gain = (f * w[i - 1, j] - fwc, f * wprev - fwc, -fwc)
                out = []
                for c in range(3):
                    one = d * here[c] + gain[c]
                    two = k[0] * ahead[c] + k[1] * v[c, i - 1, j]
                    three = k[2] * nxt[c] + k[3] * prev[c]
                    back = k[4] * here[c]
                    if c == 2:
                        back = back - fup[i, j] * wc
                    out.append((here[c], (one - two) - (three + k[4] * zp[c]) - down(back, s)))
                rows[j] = out
                ws.append((j, wc))
                prev, here, wprev, kyprev = here, nxt, wc, k[2]
            pending = emit(i, rows)
            for j, val in ws:
                w[i, j] = val
            for ref, idx, val in pending:
                ref[idx] = val
        return carry

    loop(xr[0], xr[1], body, unroll)


def loop(lo, hi, body, unroll):
    if unroll:
        for i in range(lo, hi):
            body(i, 0)
    else:
        lax.fori_loop(lo, hi, body, 0)


def smooth(v, s, xr, yr, co, w, rhs, step, out, chunk=4, unroll=False):
    def emit(i, rows):
        return [
            (out, (c, i, j), vc + step[c, i, j] * (rhs[c, i, j] - av))
            for j, vals in rows.items()
            for c, (vc, av) in enumerate(vals)
        ]

    sweep(v, s, xr, yr, co, w, emit, chunk, unroll)


def restrict(v, s, xr, yr, co, w, rhs, part, coarse, unroll=False):
    def emit(i, rows):
        pending = []
        for j in list(rows)[::2]:
            for c in range(3):
                total = (rhs[c, i, j] - rows[j][c][1]) + (rhs[c, i, j + 1] - rows[j + 1][c][1])
                pending.append((part, (c, i - xr[0], (j - yr[0]) // 2), total))
        return pending

    sweep(v, s, xr, yr, co, w, emit, 4, unroll)
    pending = []
    for c in range(3):
        for q in range((xr[1] - xr[0]) // 2):
            for y2 in range((yr[1] - yr[0]) // 2):
                pending.append(((c, q, y2), pair_sum(part[c, 2 * q, y2] + part[c, 2 * q + 1, y2], s)))
    for idx, val in pending:
        coarse[idx] = val


def pick(col, k):
    return row(col[k : k + 1, :])


def columns(m, base):
    return [row(m[:, base + k : base + k + 1]) for k in range(NC)]


def flip(a):
    out = []
    for k in range(NC):
        col = pick(a[0], k)
        for i in range(1, NC):
            col = jnp.where(subl() == i, pick(a[i], k), col)
        out.append(col)
    return out


def tree(terms):
    while len(terms) > 1:
        terms = [sum(terms[k : k + 2]) for k in range(0, len(terms), 2)]
    return terms[0]


def mm(a, b):
    return [tree([a[k] * pick(col, k) for k in range(NC)]) for col in b]


def plus(a, b):
    return [x + y for x, y in zip(a, b)]


def minus(a, b):
    return [x - y for x, y in zip(a, b)]


def solve(matrix, rhs):
    left, right = list(matrix), list(rhs)
    for k in range(NC):
        inverse = 1.0 / pick(left[k], k)
        for cols, first in ((left, k + 1), (right, 0)):
            for j in range(first, NC):
                scaled = pick(cols[j], k) * inverse
                cols[j] = jnp.where(subl() == k, scaled, cols[j] - left[k] * scaled)
    return right


def kernel(
    size_x, size_y,
    src, dens, mask, nodes, forces, xo, ro,
    eb, fb, e2b, ex, fx, e2x, e3x, one,
    g, pv, a1, a2, a3, a4, xb, w, loadbuf,
    kx, ky, kzp, fup, dm, cw, cf, ff, ad, bd,
    kx2, ky2, kzp2, fup2, dm2, cw2, cf2, ff2, ad2, bd2,
    kx3, ky3, kzp3, fup3, dm3, cw3, cf3, ff3, ad3, bd3,
    t2, g2r, x2r, ecr, g2u, b1, b2, b3, b4, w2, e2u,
    t3, g3r, g3u, c1, c2, w3,
    gram, ps1, ps2, mats, raw, part, ec0, fc0,
    send, recv, psend, precv, flat_src, fetched,
):
    gx, gy = lax.axis_index("gx"), lax.axis_index("gy")
    co1 = (kx, ky, kzp, fup, dm, cw, cf, ff, ad, bd)
    co2 = (kx2, ky2, kzp2, fup2, dm2, cw2, cf2, ff2, ad2, bd2)
    co3 = (kx3, ky3, kzp3, fup3, dm3, cw3, cf3, ff3, ad3, bd3)
    even = (lanes() & 1) == 0
    low2 = (lanes() & 2) == 0

    def valid(dx, dy):
        return (gx + dx >= 0) & (gx + dx < size_x) & (gy + dy >= 0) & (gy + dy < size_y)

    def message(kind, k, d, refs):
        a, b = refs(*d)
        return pltpu.make_async_remote_copy(
            src_ref=a, dst_ref=b, send_sem=send.at[kind, k], recv_sem=recv.at[kind, k],
            device_id=(gx + d[0], gy + d[1]), device_id_type=MESH,
        )

    def start(kind, group, refs):
        for k, d in enumerate(group):
            @pl.when(valid(*d))
            def _():
                message(kind, k, d, refs).start()

    def arrive(kind, group, refs):
        for k, d in enumerate(group):
            @pl.when(valid(-d[0], -d[1]))
            def _():
                message(kind, k, d, refs).wait_recv()

    def sent(kind, group, refs):
        for k, d in enumerate(group):
            @pl.when(valid(*d))
            def _():
                message(kind, k, d, refs).wait_send()

    def boxes(ref):
        def refs(dx, dy):
            n = NX if dx == 0 else 2 if dx == dy else 3
            at = pl.ds(NX - n if dx > 0 else 0, n)
            return ref.at[1, 1, at], ref.at[1 - dx, 1 - dy, at]
        return refs

    def e2_refs(dx, dy):
        return e2b.at[2, 1], e2b.at[2 - dx, 1 - dy]

    def halo(source, target, h, skip=0):
        def side(d, other, n):
            if d == 0:
                return 0, H, n
            near, far = (skip, h) if other == 0 else (0, h - 1 if other == d else h)
            return (n - far, H - far, far - near) if d > 0 else (near, H + n + near, far - near)

        def refs(dx, dy):
            sx, tx, nx = side(dx, dy, NX)
            sy, ty, ny = side(dy, dx, NY)
            a = source.at[:, pl.ds(H + sx, nx), pl.ds(H + sy, ny)]
            return a, target.at[:, pl.ds(tx, nx), pl.ds(ty, ny)]
        return refs

    def coarse_refs(ref):
        def refs(dx, dy):
            sy, ty, ny = span(dy, 4, 1 if dx == dy else 2, 2)
            return ref.at[:, 1, pl.ds(2 + sy, ny)], ref.at[:, 1 - dx, pl.ds(ty, ny)]
        return refs

    def g3_refs(ref):
        return lambda dx, dy: (ref.at[:, 2, 1], ref.at[:, 2 - dx, 1 - dy])

    fetch = pltpu.make_async_copy(src, flat_src, fetched)
    fetch.start()
    zero3 = jnp.zeros((NX, NY, NZ), F32)
    for bx in range(3):
        for by in range(3):
            eb[bx, by] = zero3
            fb[bx, by] = zero3
    for bx in range(5):
        for by in range(3):
            e2b[bx, by] = jnp.zeros((NC, NZ), F32)
    bar = pltpu.get_barrier_semaphore()
    corners = [(dx, dy) for dx in (1, -1, 2, -2) for dy in (1, -1)]
    peers = jnp.int32(size_x + size_y - 2)

    for d in far_first(size_x):
        pl.semaphore_signal(bar, inc=1, device_id=(lax.rem(gx + d, size_x), gy), device_id_type=MESH)
    for d in far_first(size_y):
        pl.semaphore_signal(bar, inc=1, device_id=(gx, lax.rem(gy + d, size_y)), device_id_type=MESH)
    for d in corners:
        peers = peers + jnp.where(valid(*d), 1, 0)

        @pl.when(valid(*d))
        def _():
            pl.semaphore_signal(bar, inc=1, device_id=(gx + d[0], gy + d[1]), device_id_type=MESH)
    for x in range(NX):
        rel = (dens[x].astype(F32) + 1.0) / CLASSES
        eb[1, 1, x] = MIN_MODULUS + (1.0 - MIN_MODULUS) * rel * rel * rel
        fb[1, 1, x] = 1.0 - mask[x].astype(F32)
    halves = []
    for q in range(2):
        t = eb[1, 1, 2 * q] + eb[1, 1, 2 * q + 1]
        halves.append(0.25 * pair_sum(t + pltpu.roll(t, NY - 1, 0), 1))
    e2b[2, 1] = jnp.where((subl() & 1) == 0, halves[0], pltpu.roll(halves[1], 1, 0))

    fetch.wait()
    for c in range(3):
        for x in range(NX):
            for y in range(NY):
                raw[c, H + x, H + y] = flat_src[pl.ds((c * NC * NX + x) * NY + y, NC, stride=NX * NY), :]

    pl.semaphore_wait(bar, peers)

    start(K_E, N8, boxes(eb))
    start(K_F, N8, boxes(fb))
    start(K_G, N8, halo(raw, raw, 2))
    start(K_E2, N14, e2_refs)

    def load_case(i, carry):
        node = nodes[pl.ds(i, 1), :]
        nz = lax.rem(node, NZ)
        nyx = lax.div(node, NZ)
        ny = lax.rem(nyx, size_y * NY) - gy * NY + 2
        nx = lax.div(nyx, size_y * NY) - gx * NX + 2
        hot = jnp.where(lax.broadcasted_iota(jnp.int32, (NZ, LOADS), 0) == nz, 1.0, 0.0)
        rows = lax.broadcasted_iota(jnp.int32, (16, LOADS), 0)
        parts = []
        for c in range(3):
            force = forces[c, pl.ds(i, 1), :]
            for x in range(8):
                parts.append(jnp.where((rows == ny) & (nx == x), force, 0.0))
        got = lax.dot_general(
            jnp.concatenate(parts, axis=0), hot, (((1,), (1,)), ((), ())),
            precision=lax.Precision.HIGHEST, preferred_element_type=F32,
        )
        for k in range(24):
            loadbuf[pl.ds(k * 96 + i, 8, stride=NC), :] = got[16 * k : 16 * k + 8]
            loadbuf[pl.ds(k * 96 + 64 + i, 4, stride=NC), :] = got[16 * k + 8 : 16 * k + 12]
        return carry

    lax.fori_loop(0, NC, load_case, 0)

    arrive(K_E, N8, boxes(eb))
    arrive(K_F, N8, boxes(fb))
    for i in range(AX):
        bx, xl = (i + 1) // 4, (i + 1) % 4
        for source, flat in ((eb, ec0), (fb, fc0)):
            flat[i, 0:3] = source[bx, 0, xl, 5:8]
            flat[i, 3:11] = source[bx, 1, xl]
            flat[i, 11:14] = source[bx, 2, xl, 0:3]
    compact_coefficients(ec0, fc0, co1, ex, fx)

    arrive(K_G, N8, halo(raw, raw, 2))

    def first_rhs(i, carry):
        for c in range(3):
            pending = []
            for j in range(1, 13):
                k = ((c * 8 + i - 1) * 12 + j - 1) * NC
                total = fx[i, j] * (raw[c, i, j] + loadbuf[pl.ds(pl.multiple_of(k, NC), NC), :])
                pending.append((j, jnp.where(ex[i, j] > 0.0, total, 0.0)))
            for j, val in pending:
                g[0, c, i, j] = val
        return carry

    lax.fori_loop(1, 9, first_rhs, 0)

    def unpack(p):
        return jnp.where(even, p, down(p, 1)), jnp.where(even, up(p, 1), p)

    def unpack_field(packed, out, add=None):
        for c in range(3):
            for bx in range(3):
                pending = []
                for j in range(8):
                    for a, val in enumerate(unpack(packed[c, bx, j])):
                        i = 2 * bx + a
                        val = jnp.where(ad2[0, i, j] > 0.0, val, 0.0)
                        if add is not None:
                            val = val + add[c, i // 2 + 1, j // 2 + 1]
                        pending.append(((c, i, j), val))
                for idx, val in pending:
                    out[idx] = val

    def pack_field(field, base, packed):
        for c in range(3):
            for j in range(4):
                packed[c, 1, 2 + j] = jnp.where(even, field[c, base[0], base[1] + j], field[c, base[0] + 1, base[1] + j])

    def drain(it):
        sent(K_X2 + it, N8, halo(a2, xb.at[it], 3, 1))
        sent(K_G2 + it, N8, coarse_refs(g2r.at[it]))
        sent(K_X2C + it, N8, coarse_refs(x2r.at[it]))
        sent(K_G3 + it, N14, g3_refs(g3r.at[it]))
        sent(K_EC + it, N8, coarse_refs(ecr.at[it]))

    def cycle(it, carry):
        rhs = g.at[it]
        own = ((H, H + NX), (H, H + NY))
        one_out = ((H - 1, H + NX + 1), (H - 1, H + NY + 1))
        two_out = ((H - 2, H + NX + 2), (H - 2, H + NY + 2))
        x_refs = halo(a2, xb.at[it], 3, 1)
        g2, x2, ec, g3 = g2r.at[it], x2r.at[it], ecr.at[it], g3r.at[it]

        @pl.when(it == 1)
        def _():
            def clean(i, c2_):
                for c in range(3):
                    pending = [(j, jnp.where(ex[i, j] > 0.0, rhs[c, i, j], 0.0)) for j in range(1, 13)]
                    for j, val in pending:
                        rhs[c, i, j] = val
                return c2_
            lax.fori_loop(1, 9, clean, 0)

        def first(i, c2_):
            for c in range(3):
                pending = [(j, ad[c, i, j] * rhs[c, i, j]) for j in range(1, 13)]
                for j, val in pending:
                    a1[c, i, j] = val
            return c2_

        lax.fori_loop(1, 9, first, 0)
        smooth(a1, 1, *one_out, co1, w, rhs, bd, a2, 5)
        restrict(a2, 1, *own, co1, w, rhs, part, t2)
        pack_field(t2, (0, 0), g2)
        start(K_G2 + it, N8, coarse_refs(g2))

        @pl.when(it == 0)
        def _():
            arrive(K_E2, N14, e2_refs)
            for i in range(10):
                for j in range(12):
                    k = (j % 4) * 2 + i % 2
                    e2x[i, j] = row(e2b[i // 2, j // 4, k : k + 1, :])
            for i in range(5):
                for j in range(6):
                    t = e2x[2 * i, 2 * j] + e2x[2 * i + 1, 2 * j] + e2x[2 * i, 2 * j + 1] + e2x[2 * i + 1, 2 * j + 1]
                    e3x[i, j] = 0.25 * pair_sum(t, 2)
            one[...] = jnp.ones((NC, NZ), F32)
            coefficients(
                2, lambda i, j: e2x[i + 2, j + 2], lambda i, j: one[...],
                ((0, 5), (0, 7)), ((0, 6), (0, 8)), co2,
            )
            coefficients(
                4, lambda i, j: e3x[i, j], lambda i, j: one[...],
                ((0, 4), (0, 5)), ((1, 4), (1, 5)), co3,
            )

        arrive(K_G2 + it, N8, coarse_refs(g2))
        unpack_field(g2, g2u)
        for c in range(3):
            for i in range(6):
                pending = [(j, ad2[c, i, j] * g2u[c, i, j]) for j in range(8)]
                for j, val in pending:
                    b1[c, i, j] = val
        own2, out2 = ((2, 4), (2, 6)), ((1, 5), (1, 7))
        smooth(b1, 2, *out2, co2, w2, g2u, bd2, b2, 3)
        pack_field(b2, (2, 2), x2)
        start(K_X2C + it, N8, coarse_refs(x2))
        restrict(b2, 2, *own2, co2, w2, g2u, part, t3)
        for c in range(3):
            r0, r1 = t3[c, 0, 0], t3[c, 0, 1]
            s0, s1 = ad3[c, 2, 2] * r0, ad3[c, 2, 3] * r1
            g3[c, 2, 1] = jnp.where(low2, jnp.where(even, r0, r1), jnp.where(even, s0, s1))
        start(K_G3 + it, N14, g3_refs(g3))
        start(K_X2 + it, N8, x_refs)
        arrive(K_G3 + it, N14, g3_refs(g3))
        for c in range(3):
            pending = []
            for bx in range(5):
                for by in range(3):
                    for a, q in enumerate(unpack(g3[c, bx, by])):
                        j = 2 * by + a
                        keep = e3x[bx, j] > 0.0
                        if 1 <= bx <= 3 and 1 <= j <= 4:
                            pending.append((g3u, (c, bx, j), jnp.where(keep, jnp.where(low2, q, down(q, 2)), 0.0)))
                        pending.append((c1, (c, bx, j), jnp.where(keep, jnp.where(low2, up(q, 2), q), 0.0)))
            for ref, idx, val in pending:
                ref[idx] = val
        smooth(c1, 4, (1, 4), (1, 5), co3, w3, g3u, bd3, c2, 4)
        arrive(K_X2C + it, N8, coarse_refs(x2))
        unpack_field(x2, b3, add=c2)
        smooth(b3, 2, *out2, co2, w2, g2u, bd2, b4, 3)
        smooth(b4, 2, *own2, co2, w2, g2u, ad2, b1, 4)
        pack_field(b1, (2, 2), ec)
        start(K_EC + it, N8, coarse_refs(ec))
        arrive(K_EC + it, N8, coarse_refs(ec))
        unpack_field(ec, e2u)
        arrive(K_X2 + it, N8, x_refs)

        def correct(i, from_own):
            for c in range(3):
                pending = []
                for j in range(AY):
                    inner = from_own(j)
                    old = a2[c, i, j] if inner else xb[it, c, i, j]
                    keep = ex[i, j] > 0.0
                    e = e2u[c, (i + 1) // 2, (j + 1) // 2]
                    pending.append((j, jnp.where(keep, old + fx[i, j] * e, 0.0)))
                for j, val in pending:
                    a3[c, i, j] = val

        for i in range(AX):
            out = 0 if H <= i < H + NX else 1 if H - 1 <= i <= H + NX else 9
            correct(i, lambda j: out + (not H <= j < H + NY) + 9 * (not H - 1 <= j <= H + NY) < 2)
        smooth(a3, 1, *two_out, co1, w, rhs, bd, a4)
        smooth(a4, 1, *one_out, co1, w, rhs, ad, pv.at[it], 5)

        def keep_image(i, rows):
            return [(g, (it + 1, c, i, j), av) for j, vals in rows.items() for c, (_, av) in enumerate(vals)]

        sweep(pv.at[it], 1, *own, co1, w, keep_image, 4, False)

        q_refs = halo(g.at[1], g.at[1], 2)

        @pl.when(it == 0)
        def _():
            start(K_G + 1, N8, q_refs)

        def gram_plane(i, accs):
            accs = list(accs)
            for c in range(3):
                for j in range(H, H + NY):
                    left = [g[q, c, i, j] for q in range(2)] + [jnp.where(it == 1, g[2, c, i, j], 0.0)]
                    for k in range(NC):
                        right = row(pv[it, c, i, j, k : k + 1, :])
                        for q in range(3):
                            accs[q * NC + k] = accs[q * NC + k] + left[q] * right
            return tuple(accs)

        zeros = tuple(jnp.zeros((NC, NZ), F32) for _ in range(3 * NC))
        accs = lax.fori_loop(H, H + NX, gram_plane, zeros)
        out = jnp.zeros((NC, NZ), F32)
        for q in range(3):
            for k in range(NC):
                out = jnp.where(lanes() == q * NC + k, row(jnp.sum(accs[q * NC + k], axis=1, keepdims=True)), out)
        gram[it] = out

        @pl.when(it == 0)
        def _():
            drain(0)
            arrive(K_G + 1, N8, q_refs)
            sent(K_G + 1, N8, q_refs)

        return carry

    lax.fori_loop(0, 2, cycle, 0)

    def settle():
        drain(1)
        sent(K_E, N8, boxes(eb))
        sent(K_F, N8, boxes(fb))
        sent(K_G, N8, halo(raw, raw, 2))
        sent(K_E2, N14, e2_refs)

    def total(buffer, me, count, place, base, meanwhile=None):
        def copy(d):
            return pltpu.make_async_remote_copy(
                src_ref=buffer.at[me], dst_ref=buffer.at[me],
                send_sem=psend.at[base + d], recv_sem=precv.at[base + me],
                device_id=place(lax.rem(me + d, count)), device_id_type=MESH,
            )

        def landing(d):
            other = lax.rem(me + d, count)
            return pltpu.make_async_remote_copy(
                src_ref=buffer.at[other], dst_ref=buffer.at[other],
                send_sem=psend.at[base + d], recv_sem=precv.at[base + other],
                device_id=place(other), device_id_type=MESH,
            )

        for d in far_first(count):
            copy(d).start()
        if meanwhile is not None:
            meanwhile()
        for d in far_first(count)[::-1]:
            landing(d).wait_recv()
        for d in range(1, count):
            copy(d).wait_send()
        out = buffer[0]
        for k in range(1, count):
            out = out + buffer[k]
        return out

    ps1[gy] = jnp.where(lanes() < 2 * NC, gram[0], pltpu.roll(gram[1], 2 * NC, 1))
    ps2[gx] = total(ps1, gy, size_y, lambda k: (gx, k), 0, settle)
    sums = total(ps2, gx, size_x, lambda k: (k, gy), size_y)

    rz = columns(sums, 0)
    qp = columns(sums, NC)
    ru = columns(sums, 2 * NC)
    qu = columns(sums, 3 * NC)
    wu = columns(sums, 4 * NC)
    alpha = solve(qp, rz)
    alpha_t = flip(alpha)
    qua = mm(qu, alpha)
    rz2 = plus(minus(rz, mm(ru, alpha)), mm(alpha_t, minus(qua, qp)))
    mix = [jnp.where(subl() == k, col + 1.0, col) for k, col in enumerate(solve(rz, rz2))]
    ahead = minus(mm(flip(qp), mix), qua)
    behind = minus(mm(flip(wu), alpha), mm(flip(qu), mix))
    alpha2 = solve(plus(mm(flip(mix), ahead), mm(alpha_t, behind)), rz2)
    for q, m in enumerate((plus(alpha, mm(mix, alpha2)), mm(alpha, alpha2))):
        for k, col in enumerate(flip(m)):
            mats[q, k] = col

    def finish(n, carry):
        c, x = lax.div(n, NX), lax.rem(n, NX)
        i = H + x
        for one, two, ref, base in ((pv.at[0], pv.at[1], xo, None), (g.at[1], g.at[2], ro, g.at[0])):
            accs = [None] * NY
            for k in range(NC):
                m1, m2 = mats[0, k], mats[1, k]
                for y in range(NY):
                    j = H + y
                    term = row(one[c, i, j, k : k + 1, :]) * m1 - row(two[c, i, j, k : k + 1, :]) * m2
                    accs[y] = term if k == 0 else accs[y] + term
            pending = [(y, acc if base is None else base[c, i, H + y] - acc) for y, acc in enumerate(accs)]
            for y, val in pending:
                ref[pl.ds((c * NC * NX + x) * NY + y, NC, stride=NX * NY), :] = val
        return carry

    lax.fori_loop(0, 3 * NX, finish, 0)


def publish(a, b, out_a, out_b, stage, sem):
    loads, stores = [], []
    n = a.shape[0] // PIECES
    for k in range(PIECES):
        for q, (one, two) in enumerate(((a, out_a), (b, out_b))):
            at = pl.ds(k * n, n)
            loads.append(pltpu.make_async_copy(one.at[at], stage.at[q, at], sem.at[0, q, k]))
            stores.append(pltpu.make_async_copy(stage.at[q, at], two.at[at], sem.at[1, q, k]))
    for copy in loads:
        copy.start()
    for load, store in zip(loads, stores):
        load.wait()
        store.start()
    for copy in stores:
        copy.wait()


def on_device(size_x, size_y, source_field, density_class, fixed_mask, load_nodes, load_forces):
    rows = 3 * NC * NX * NY
    tile = (NC, NZ)

    def vm(*dims):
        return pltpu.VMEM(dims + tile, F32)

    def level(nx, ny):
        return [vm(nx, ny)] * 5 + [vm(3, nx, ny), vm(nx, ny), vm(nx, ny), vm(3, nx, ny), vm(3, nx, ny)]

    scratch = [
        pltpu.VMEM((3, 3, NX, NY, NZ), F32), pltpu.VMEM((3, 3, NX, NY, NZ), F32), vm(5, 3),
        vm(AX, AY), vm(AX, AY), vm(10, 12), vm(5, 6), vm(),
        vm(3, 3, AX, AY), vm(2, 3, AX, AY), vm(3, AX, AY), vm(3, AX, AY), vm(3, AX, AY), vm(3, AX, AY),
        vm(2, 3, AX, AY), vm(AX, AY), pltpu.VMEM((3 * 8 * 12 * NC, NZ), F32),
    ]
    scratch += level(AX, AY) + level(6, 8) + level(5, 6)
    scratch += [vm(3, 2, 4), vm(2, 3, 3, 8), vm(2, 3, 3, 8), vm(2, 3, 3, 8)]
    scratch += [vm(3, 6, 8)] * 5 + [vm(6, 8), vm(3, 6, 8)]
    scratch += [vm(3, 1, 2), vm(2, 3, 5, 3), vm(3, 5, 6), vm(3, 5, 6), vm(3, 5, 6), vm(5, 6)]
    scratch += [vm(2), vm(size_y), vm(size_x), vm(2, NC), vm(3, AX, AY), vm(3, NX, 4)]
    scratch += [pltpu.VMEM((AX, 16, NZ), F32)] * 2
    sems = pltpu.SemaphoreType.DMA
    scratch += [sems((KINDS, len(N14))), sems((KINDS, len(N14))), sems((size_x + size_y,)), sems((size_x + size_y,))]
    scratch += [pltpu.VMEM((rows, NZ), F32), sems(())]
    spec = pl.BlockSpec(memory_space=pltpu.VMEM)
    shape = jax.ShapeDtypeStruct((rows, NZ), F32)
    sol, res = pl.pallas_call(
        functools.partial(kernel, size_x, size_y),
        out_shape=(shape, shape),
        in_specs=[pl.BlockSpec(memory_space=pl.ANY)] + [spec] * 4,
        out_specs=(spec, spec),
        scratch_shapes=scratch,
        compiler_params=pltpu.CompilerParams(
            collective_id=0, has_side_effects=True, vmem_limit_bytes=56 * 1024 * 1024
        ),
        name="block_pcg",
    )(source_field.reshape(rows, NZ), density_class, fixed_mask, load_nodes, load_forces)
    whole = pl.BlockSpec(memory_space=pl.ANY)
    sol, res = pl.pallas_call(
        publish,
        out_shape=(shape, shape),
        in_specs=[whole] * 2,
        out_specs=(whole, whole),
        scratch_shapes=[pltpu.VMEM((2, rows, NZ), F32), sems((2, 2, PIECES))],
        name="publish",
    )(sol, res)
    return sol.reshape(source_field.shape), res.reshape(source_field.shape)


def solution(mesh):
    placed = (P(None, None, "gx", "gy", None), P("gx", "gy", None), P("gx", "gy", None), P(), P())
    return jax.shard_map(
        functools.partial(on_device, mesh.shape["gx"], mesh.shape["gy"]),
        mesh=mesh,
        in_specs=placed,
        out_specs=(P(None, None, "gx", "gy", None), P(None, None, "gx", "gy", None)),
        check_vma=False,
    )
```

```python
import functools
import math

import jax
import jax.numpy as jnp
from jax import lax
from jax.experimental import pallas as pl
from jax.experimental.pallas import tpu as pltpu
from jax.sharding import PartitionSpec as P

CLASSES = 16
MU = 1.0 / 2.6
LAM = 0.3 / 0.52
MIN_MODULUS = 0.05
STEP_A = 1.0 / (2.7 + 2.1 * math.cos(math.pi / 4.0))
STEP_B = 1.0 / (2.7 - 2.1 * math.cos(math.pi / 4.0))
MESH = pl.DeviceIdType.MESH
F32 = jnp.float32

NX, NY, NC, NZ, LOADS = 4, 8, 8, 128, 64
NROWS = 3 * NC * NX * NY
H = 3
AX, AY = NX + 2 * H, NY + 2 * H
N8 = [(1, -1), (-1, 1), (1, 1), (-1, -1), (1, 0), (-1, 0), (0, 1), (0, -1)]
N14 = [(dx, dy) for dx in (2, -2, 1, -1, 0) for dy in (1, -1, 0) if (dx, dy) != (0, 0)]

K_E, K_F, K_E2, K_G, K_X2, K_G2, K_X2C, K_G3, K_EC = 0, 1, 2, 3, 5, 7, 9, 11, 13
KINDS = 15
PIECES = 4


def far_first(count):
    return sorted(range(1, count), key=lambda d: abs(d - count / 2))


def lanes():
    return lax.broadcasted_iota(jnp.int32, (NC, NZ), 1)


def subl():
    return lax.broadcasted_iota(jnp.int32, (NC, NZ), 0)


def up(v, s):
    return pltpu.roll(v, NZ - s, 1)


def down(v, s):
    return pltpu.roll(v, s, 1)


def pair_sum(v, s):
    other = jnp.where((lanes() & s) == 0, up(v, s), down(v, s))
    return v + other


def row(v):
    return jnp.broadcast_to(v, (NC, NZ))


def span(d, n, h, base):
    if d > 0:
        return n - h, base - h, h
    if d < 0:
        return 0, base + n, h
    return 0, base, n


def coefficients(s, e_at, f_at, low, inv, co, unroll=False):
    kx, ky, kzp, fup, dm, cw, cf, ff, ad, bd = co
    last = lanes() >= NZ - s
    first = lanes() < s
    half = 0.5 * MU

    def lower(i, carry):
        pending = []
        for j in range(*low[1]):
            e, f = e_at(i, j), f_at(i, j)
            fx, fy = f_at(i + 1, j), f_at(i, j + 1)
            fzp = jnp.where(last, 0.0, up(f, s))
            ezp = up(e, s)
            le = LAM * e
            hf = half * f
            pending += [
                (kx, (i, j), (e + e_at(i + 1, j)) * (hf * fx)),
                (ky, (i, j), (e + e_at(i, j + 1)) * (hf * fy)),
                (kzp, (i, j), (e + ezp) * (hf * fzp)),
                (fup, (i, j), fzp),
                (cw, (0, i, j), le * fx),
                (cw, (1, i, j), le * fy),
                (cw, (2, i, j), le * fzp),
                (cf, (i, j), le * f),
                (ff, (i, j), f),
            ]
            if j % 3 == 2 or j == low[1][1] - 1:
                for ref, idx, val in pending:
                    ref[idx] = val
                pending = []
        return carry

    loop(low[0][0], low[0][1], lower, unroll)

    def smoother(i, carry):
        pending = []
        for j in range(*inv[1]):
            e, f = e_at(i, j), f_at(i, j)
            ezp = jnp.where(last, 0.0, up(e, s))
            ezm = jnp.where(first, 0.0, down(e, s))
            ex, ey = e_at(i - 1, j), e_at(i, j - 1)
            d = half * (ex + e_at(i + 1, j) + ey + e_at(i, j + 1) + ezm + ezp + 6.0 * e)
            pending.append((dm, (i, j), f * d + (1.0 - f)))
            for c, below in enumerate((ex, ey, ezm)):
                diag = jnp.where(e > 0.0, d + LAM * (e + below), 1.0)
                dinv = jnp.where(e > 0.0, f / diag + (1.0 - f), 0.0)
                pending.append((ad, (c, i, j), STEP_A * dinv))
                pending.append((bd, (c, i, j), STEP_B * dinv))
            if j % 3 == 2 or j == inv[1][1] - 1:
                for ref, idx, val in pending:
                    ref[idx] = val
                pending = []
        return carry

    loop(inv[0][0], inv[0][1], smoother, unroll)


def compact_coefficients(e_ref, f_ref, co, ex, fx):
    kx, ky, kzp, fup, dm, cw, cf, ff, ad, bd = co
    half = 0.5 * MU
    wide = (16, NZ)
    lane = lax.broadcasted_iota(jnp.int32, wide, 1)

    def zup(v):
        return jnp.where(lane == NZ - 1, 0.0, pltpu.roll(v, NZ - 1, 1))

    def ynext(v):
        return pltpu.roll(v, 15, 0)

    def plane(i, carry):
        e, f, e1, f1 = e_ref[i], f_ref[i], e_ref[i + 1], f_ref[i + 1]
        fy, fz = ynext(f), zup(f)
        le, hf = LAM * e, half * f
        ahead = (
            (ex, (i,), e), (fx, (i,), f),
            (kx, (i,), (e + e1) * (hf * f1)),
            (ky, (i,), (e + ynext(e)) * (hf * fy)),
            (kzp, (i,), (e + zup(e)) * (hf * fz)),
            (fup, (i,), fz), (cw, (0, i), le * f1), (cw, (1, i), le * fy),
            (cw, (2, i), le * fz), (cf, (i,), le * f), (ff, (i,), f),
        )
        for ref, at, val in ahead:
            for j in range(AY):
                ref[at + (j,)] = row(val[j : j + 1, :])
        return carry

    lax.fori_loop(0, AX - 1, plane, 0)
    for ref, source in ((ex, e_ref), (fx, f_ref)):
        last = source[AX - 1]
        for j in range(AY):
            ref[AX - 1, j] = row(last[j : j + 1, :])

    def smoother(i, carry):
        e, f = e_ref[i], f_ref[i]
        ey = pltpu.roll(e, 1, 0)
        ez = jnp.where(lane == 0, 0.0, pltpu.roll(e, 1, 1))
        eb = e_ref[i - 1]
        d = half * (eb + e_ref[i + 1] + ey + ynext(e) + ez + zup(e) + 6.0 * e)
        out = [(dm, (i,), f * d + (1.0 - f))]
        for c, below in enumerate((eb, ey, ez)):
            diag = jnp.where(e > 0.0, d + LAM * (e + below), 1.0)
            dinv = jnp.where(e > 0.0, f / diag + (1.0 - f), 0.0)
            out += [(ad, (c, i), STEP_A * dinv), (bd, (c, i), STEP_B * dinv)]
        for ref, at, val in out:
            for j in range(1, AY - 1):
                ref[at + (j,)] = row(val[j : j + 1, :])
        return carry

    lax.fori_loop(1, AX - 1, smoother, 0)


def sweep(v, s, xr, yr, co, w, emit, chunk, unroll):
    kx, ky, kzp, fup, dm, cw, cf, ff = co[:8]

    def spread(i, j, centre, ahead_x, ahead_y, ahead_z):
        total = centre[0] + centre[1] + centre[2]
        return cw[0, i, j] * ahead_x + cw[1, i, j] * ahead_y + cw[2, i, j] * ahead_z - cf[i, j] * total

    def at(i, j):
        return [v[c, i, j] for c in range(3)]

    before = xr[0] - 1
    stores = []
    for j in range(*yr):
        centre = at(before, j)
        stores.append((j, spread(before, j, centre, v[0, before + 1, j], v[1, before, j + 1], up(centre[2], s))))
    for j, val in stores:
        w[before, j] = val

    def body(i, carry):
        j0 = yr[0] - 1
        prev = at(i, j0)
        here = at(i, yr[0])
        wprev = spread(i, j0, prev, v[0, i + 1, j0], here[1], up(prev[2], s))
        kyprev = ky[i, j0]
        for ja in range(yr[0], yr[1], chunk):
            rows, ws = {}, []
            for j in range(ja, min(ja + chunk, yr[1])):
                nxt = at(i, j + 1)
                ahead = [v[c, i + 1, j] for c in range(3)]
                zp = [up(here[c], s) for c in range(3)]
                wc = spread(i, j, here, ahead[0], nxt[1], zp[2])
                k = (kx[i, j], kx[i - 1, j], ky[i, j], kyprev, kzp[i, j])
                f, d = ff[i, j], dm[i, j]
                fwc = f * wc
                gain = (f * w[i - 1, j] - fwc, f * wprev - fwc, -fwc)
                out = []
                for c in range(3):
                    one = d * here[c] + gain[c]
                    two = k[0] * ahead[c] + k[1] * v[c, i - 1, j]
                    three = k[2] * nxt[c] + k[3] * prev[c]
                    back = k[4] * here[c]
                    if c == 2:
                        back = back - fup[i, j] * wc
                    out.append((here[c], (one - two) - (three + k[4] * zp[c]) - down(back, s)))
                rows[j] = out
                ws.append((j, wc))
                prev, here, wprev, kyprev = here, nxt, wc, k[2]
            pending = emit(i, rows)
            for j, val in ws:
                w[i, j] = val
            for ref, idx, val in pending:
                ref[idx] = val
        return carry

    loop(xr[0], xr[1], body, unroll)


def loop(lo, hi, body, unroll):
    if unroll:
        for i in range(lo, hi):
            body(i, 0)
    else:
        lax.fori_loop(lo, hi, body, 0)


def smooth(v, s, xr, yr, co, w, rhs, step, out, chunk=4, unroll=False):
    def emit(i, rows):
        return [
            (out, (c, i, j), vc + step[c, i, j] * (rhs[c, i, j] - av))
            for j, vals in rows.items()
            for c, (vc, av) in enumerate(vals)
        ]

    sweep(v, s, xr, yr, co, w, emit, chunk, unroll)


def restrict(v, s, xr, yr, co, w, rhs, part, coarse, unroll=False):
    def emit(i, rows):
        pending = []
        for j in list(rows)[::2]:
            for c in range(3):
                total = (rhs[c, i, j] - rows[j][c][1]) + (rhs[c, i, j + 1] - rows[j + 1][c][1])
                pending.append((part, (c, i - xr[0], (j - yr[0]) // 2), total))
        return pending

    sweep(v, s, xr, yr, co, w, emit, 4, unroll)
    pending = []
    for c in range(3):
        for q in range((xr[1] - xr[0]) // 2):
            for y2 in range((yr[1] - yr[0]) // 2):
                pending.append(((c, q, y2), pair_sum(part[c, 2 * q, y2] + part[c, 2 * q + 1, y2], s)))
    for idx, val in pending:
        coarse[idx] = val


def pick(m, k):
    return row(m[k : k + 1, :])


def columns(m):
    return [row(m[:, k : k + 1]) for k in range(NC)]


def flipped(m):
    diagonal = lanes() == subl()
    return [row(jnp.sum(jnp.where(diagonal, pick(m, k), 0.0), axis=1, keepdims=True)) for k in range(NC)]


def tree(terms):
    while len(terms) > 1:
        terms = [sum(terms[k : k + 2]) for k in range(0, len(terms), 2)]
    return terms[0]


def mm(cols, m):
    return tree([cols[k] * pick(m, k) for k in range(NC)])


def solve(cols, rhs):
    left = list(cols)
    for k in range(NC):
        pivot_row = subl() == k
        inverse = 1.0 / pick(left[k], k)
        for j in range(k + 1, NC):
            scaled = pick(left[j], k) * inverse
            left[j] = jnp.where(pivot_row, scaled, left[j] - left[k] * scaled)
        scaled = pick(rhs, k) * inverse
        rhs = jnp.where(pivot_row, scaled, rhs - left[k] * scaled)
    return rhs


def kernel(
    size_x, size_y,
    src, dens_in, mask_in, nodes_in, forces_in, xo, ro,
    eb, fb, e2b, ex, fx, e2x, e3x, one,
    g, pv, a1, a2, a3, a4, xb, w, loadbuf,
    kx, ky, kzp, fup, dm, cw, cf, ff, ad, bd,
    kx2, ky2, kzp2, fup2, dm2, cw2, cf2, ff2, ad2, bd2,
    kx3, ky3, kzp3, fup3, dm3, cw3, cf3, ff3, ad3, bd3,
    t2, g2r, x2r, ecr, g2u, b1, b2, b3, b4, w2, e2u,
    t3, g3r, g3u, c1, c2, w3,
    gram, ps1, ps2, mats, raw, pairs, ec0, fc0,
    send, recv, psend, precv, flat_src, stage, stored, dens, mask, nodes, forces, fetched,
):
    gx, gy = lax.axis_index("gx"), lax.axis_index("gy")
    co1 = (kx, ky, kzp, fup, dm, cw, cf, ff, ad, bd)
    co2 = (kx2, ky2, kzp2, fup2, dm2, cw2, cf2, ff2, ad2, bd2)
    co3 = (kx3, ky3, kzp3, fup3, dm3, cw3, cf3, ff3, ad3, bd3)
    even = (lanes() & 1) == 0
    low2 = (lanes() & 2) == 0

    def valid(dx, dy):
        return (gx + dx >= 0) & (gx + dx < size_x) & (gy + dy >= 0) & (gy + dy < size_y)

    def message(kind, k, d, refs):
        a, b = refs(*d)
        return pltpu.make_async_remote_copy(
            src_ref=a, dst_ref=b, send_sem=send.at[kind, k], recv_sem=recv.at[kind, k],
            device_id=(gx + d[0], gy + d[1]), device_id_type=MESH,
        )

    def start(kind, group, refs):
        for k, d in enumerate(group):
            @pl.when(valid(*d))
            def _():
                message(kind, k, d, refs).start()

    def arrive(kind, group, refs):
        for k, d in enumerate(group):
            @pl.when(valid(-d[0], -d[1]))
            def _():
                message(kind, k, d, refs).wait_recv()

    def sent(kind, group, refs):
        for k, d in enumerate(group):
            @pl.when(valid(*d))
            def _():
                message(kind, k, d, refs).wait_send()

    def boxes(ref):
        def refs(dx, dy):
            n = NX if dx == 0 else 2 if dx == dy else 3
            at = pl.ds(NX - n if dx > 0 else 0, n)
            return ref.at[1, 1, at], ref.at[1 - dx, 1 - dy, at]
        return refs

    def e2_refs(dx, dy):
        return e2b.at[2, 1], e2b.at[2 - dx, 1 - dy]

    def halo(source, target, h, skip=0):
        def side(d, other, n):
            if d == 0:
                return 0, H, n
            near, far = (skip, h) if other == 0 else (0, h - 1 if other == d else h)
            return (n - far, H - far, far - near) if d > 0 else (near, H + n + near, far - near)

        def refs(dx, dy):
            sx, tx, nx = side(dx, dy, NX)
            sy, ty, ny = side(dy, dx, NY)
            a = source.at[:, pl.ds(H + sx, nx), pl.ds(H + sy, ny)]
            return a, target.at[:, pl.ds(tx, nx), pl.ds(ty, ny)]
        return refs

    def coarse_refs(ref):
        def refs(dx, dy):
            sy, ty, ny = span(dy, 4, 1 if dx == dy else 2, 2)
            return ref.at[:, 1, pl.ds(2 + sy, ny)], ref.at[:, 1 - dx, pl.ds(ty, ny)]
        return refs

    def g3_refs(ref):
        return lambda dx, dy: (ref.at[:, 2, 1], ref.at[:, 2 - dx, 1 - dy])

    inputs = ((dens_in, dens), (mask_in, mask), (src, flat_src.at[pl.ds(0, NROWS)]), (nodes_in, nodes), (forces_in, forces))
    fetch = [pltpu.make_async_copy(a, b, fetched.at[k]) for k, (a, b) in enumerate(inputs)]
    for copy in fetch:
        copy.start()
    zero3 = jnp.zeros((NX, NY, NZ), F32)
    for bx in range(3):
        for by in range(3):
            eb[bx, by] = zero3
            fb[bx, by] = zero3
    for bx in range(5):
        for by in range(3):
            e2b[bx, by] = jnp.zeros((NC, NZ), F32)
    bar = pltpu.get_barrier_semaphore()
    corners = [(dx, dy) for dx in (1, -1, 2, -2) for dy in (1, -1)]
    peers = jnp.int32(size_x + size_y - 2)

    for d in far_first(size_x):
        pl.semaphore_signal(bar, inc=1, device_id=(lax.rem(gx + d, size_x), gy), device_id_type=MESH)
    for d in far_first(size_y):
        pl.semaphore_signal(bar, inc=1, device_id=(gx, lax.rem(gy + d, size_y)), device_id_type=MESH)
    for d in corners:
        peers = peers + jnp.where(valid(*d), 1, 0)

        @pl.when(valid(*d))
        def _():
            pl.semaphore_signal(bar, inc=1, device_id=(gx + d[0], gy + d[1]), device_id_type=MESH)
    fetch[0].wait()
    fetch[1].wait()
    for x in range(NX):
        rel = (dens[x].astype(F32) + 1.0) / CLASSES
        eb[1, 1, x] = MIN_MODULUS + (1.0 - MIN_MODULUS) * rel * rel * rel
        fb[1, 1, x] = 1.0 - mask[x].astype(F32)
    halves = []
    for q in range(2):
        t = eb[1, 1, 2 * q] + eb[1, 1, 2 * q + 1]
        halves.append(0.25 * pair_sum(t + pltpu.roll(t, NY - 1, 0), 1))
    e2b[2, 1] = jnp.where((subl() & 1) == 0, halves[0], pltpu.roll(halves[1], 1, 0))

    fetch[2].wait()
    for c in range(3):
        for x in range(NX):
            for y in range(NY):
                raw[c, H + x, H + y] = flat_src[pl.ds((c * NC * NX + x) * NY + y, NC, stride=NX * NY), :]

    pl.semaphore_wait(bar, peers)

    start(K_E, N8, boxes(eb))
    start(K_F, N8, boxes(fb))
    start(K_G, N8, halo(raw, raw, 2))
    start(K_E2, N14, e2_refs)

    def load_case(i, carry):
        node = nodes[pl.ds(i, 1), :]
        nz = lax.rem(node, NZ)
        nyx = lax.div(node, NZ)
        ny = lax.rem(nyx, size_y * NY) - gy * NY + 2
        nx = lax.div(nyx, size_y * NY) - gx * NX + 2
        hot = jnp.where(lax.broadcasted_iota(jnp.int32, (NZ, LOADS), 0) == nz, 1.0, 0.0)
        rows = lax.broadcasted_iota(jnp.int32, (16, LOADS), 0)
        parts = []
        for c in range(3):
            force = forces[c, pl.ds(i, 1), :]
            for x in range(8):
                parts.append(jnp.where((rows == ny) & (nx == x), force, 0.0))
        got = lax.dot_general(
            jnp.concatenate(parts, axis=0), hot, (((1,), (1,)), ((), ())),
            precision=lax.Precision.HIGHEST, preferred_element_type=F32,
        )
        for k in range(24):
            loadbuf[pl.ds(k * 96 + i, 8, stride=NC), :] = got[16 * k : 16 * k + 8]
            loadbuf[pl.ds(k * 96 + 64 + i, 4, stride=NC), :] = got[16 * k + 8 : 16 * k + 12]
        return carry

    fetch[3].wait()
    fetch[4].wait()
    lax.fori_loop(0, NC, load_case, 0)

    arrive(K_E, N8, boxes(eb))
    arrive(K_F, N8, boxes(fb))
    for i in range(AX):
        bx, xl = (i + 1) // 4, (i + 1) % 4
        for source, flat in ((eb, ec0), (fb, fc0)):
            flat[i, 0:3] = source[bx, 0, xl, 5:8]
            flat[i, 3:11] = source[bx, 1, xl]
            flat[i, 11:14] = source[bx, 2, xl, 0:3]
    compact_coefficients(ec0, fc0, co1, ex, fx)

    arrive(K_G, N8, halo(raw, raw, 2))

    def first_rhs(i, carry):
        for c in range(3):
            pending = []
            for j in range(1, 13):
                k = ((c * 8 + i - 1) * 12 + j - 1) * NC
                total = fx[i, j] * (raw[c, i, j] + loadbuf[pl.ds(pl.multiple_of(k, NC), NC), :])
                total = jnp.where(ex[i, j] > 0.0, total, 0.0)
                pending.append((j, total, ad[c, i, j] * total))
            for j, val, step in pending:
                g[0, c, i, j] = val
                a1[c, i, j] = step
        return carry

    lax.fori_loop(1, 9, first_rhs, 0)

    def unpack(p):
        return jnp.where(even, p, down(p, 1)), jnp.where(even, up(p, 1), p)

    def unpack_field(packed, out, own, base, add=None):
        for c in range(3):
            for bx in range(3):
                pending = []
                for j in range(1 if bx == 0 else 0, 7 if bx == 2 else 8):
                    inner = bx == 1 and 2 <= j < 6
                    both = [own[c, base + a, base + j - 2] for a in range(2)] if inner else unpack(packed[c, bx, j])
                    for a, val in enumerate(both):
                        i = 2 * bx + a
                        if not inner:
                            val = jnp.where(ad2[0, i, j] > 0.0, val, 0.0)
                        if add is not None:
                            val = val + add[c, i // 2 + 1, j // 2 + 1]
                        pending.append(((c, i, j), val))
                for idx, val in pending:
                    out[idx] = val

    def pack_field(field, base, packed):
        for c in range(3):
            for j in range(4):
                packed[c, 1, 2 + j] = jnp.where(even, field[c, base[0], base[1] + j], field[c, base[0] + 1, base[1] + j])

    def drain(it):
        sent(K_X2 + it, N8, halo(a2, xb.at[it], 3, 1))
        sent(K_G2 + it, N8, coarse_refs(g2r.at[it]))
        sent(K_X2C + it, N8, coarse_refs(x2r.at[it]))
        sent(K_G3 + it, N14, g3_refs(g3r.at[it]))
        sent(K_EC + it, N8, coarse_refs(ecr.at[it]))

    def cycle(it, carry):
        rhs = g.at[it]
        own = ((H, H + NX), (H, H + NY))
        one_out = ((H - 1, H + NX + 1), (H - 1, H + NY + 1))
        two_out = ((H - 2, H + NX + 2), (H - 2, H + NY + 2))
        x_refs = halo(a2, xb.at[it], 3, 1)
        g2, x2, ec, g3 = g2r.at[it], x2r.at[it], ecr.at[it], g3r.at[it]

        @pl.when(it == 1)
        def _():
            def clean(i, c2_):
                for c in range(3):
                    pending = [(j, jnp.where(ex[i, j] > 0.0, rhs[c, i, j], 0.0)) for j in range(1, 13)]
                    pending = [(j, val, ad[c, i, j] * val) for j, val in pending]
                    for j, val, step in pending:
                        rhs[c, i, j] = val
                        a1[c, i, j] = step
                return c2_
            lax.fori_loop(1, 9, clean, 0)

        smooth(a1, 1, *one_out, co1, w, rhs, bd, a2, 5)
        restrict(a2, 1, *own, co1, w, rhs, pairs, t2)
        pack_field(t2, (0, 0), g2)
        start(K_G2 + it, N8, coarse_refs(g2))

        @pl.when(it == 0)
        def _():
            arrive(K_E2, N14, e2_refs)
            for i in range(10):
                for j in range(12):
                    k = (j % 4) * 2 + i % 2
                    e2x[i, j] = row(e2b[i // 2, j // 4, k : k + 1, :])
            for i in range(5):
                for j in range(6):
                    t = e2x[2 * i, 2 * j] + e2x[2 * i + 1, 2 * j] + e2x[2 * i, 2 * j + 1] + e2x[2 * i + 1, 2 * j + 1]
                    e3x[i, j] = 0.25 * pair_sum(t, 2)
            one[...] = jnp.ones((NC, NZ), F32)
            coefficients(
                2, lambda i, j: e2x[i + 2, j + 2], lambda i, j: one[...],
                ((0, 5), (0, 7)), ((0, 6), (0, 8)), co2,
            )
            coefficients(
                4, lambda i, j: e3x[i, j], lambda i, j: one[...],
                ((0, 4), (0, 5)), ((1, 4), (1, 5)), co3,
            )

        arrive(K_G2 + it, N8, coarse_refs(g2))
        unpack_field(g2, g2u, t2, 0)
        for c in range(3):
            for i in range(6):
                pending = [(j, ad2[c, i, j] * g2u[c, i, j]) for j in range(8)]
                for j, val in pending:
                    b1[c, i, j] = val
        own2, out2 = ((2, 4), (2, 6)), ((1, 5), (1, 7))
        smooth(b1, 2, *out2, co2, w2, g2u, bd2, b2, 3)
        pack_field(b2, (2, 2), x2)
        start(K_X2C + it, N8, coarse_refs(x2))
        restrict(b2, 2, *own2, co2, w2, g2u, pairs, t3)
        for c in range(3):
            r0, r1 = t3[c, 0, 0], t3[c, 0, 1]
            s0, s1 = ad3[c, 2, 2] * r0, ad3[c, 2, 3] * r1
            g3[c, 2, 1] = jnp.where(low2, jnp.where(even, r0, r1), jnp.where(even, s0, s1))
        start(K_G3 + it, N14, g3_refs(g3))
        start(K_X2 + it, N8, x_refs)
        arrive(K_G3 + it, N14, g3_refs(g3))
        for c in range(3):
            pending = []
            for bx in range(5):
                for by in range(3):
                    for a, q in enumerate(unpack(g3[c, bx, by])):
                        j = 2 * by + a
                        keep = e3x[bx, j] > 0.0
                        if 1 <= bx <= 3 and 1 <= j <= 4:
                            pending.append((g3u, (c, bx, j), jnp.where(keep, jnp.where(low2, q, down(q, 2)), 0.0)))
                        pending.append((c1, (c, bx, j), jnp.where(keep, jnp.where(low2, up(q, 2), q), 0.0)))
            for ref, idx, val in pending:
                ref[idx] = val
        smooth(c1, 4, (1, 4), (1, 5), co3, w3, g3u, bd3, c2, 4)
        arrive(K_X2C + it, N8, coarse_refs(x2))
        unpack_field(x2, b3, b2, 2, add=c2)
        smooth(b3, 2, *out2, co2, w2, g2u, bd2, b4, 3)
        smooth(b4, 2, *own2, co2, w2, g2u, ad2, b1, 4)
        pack_field(b1, (2, 2), ec)
        start(K_EC + it, N8, coarse_refs(ec))
        arrive(K_EC + it, N8, coarse_refs(ec))
        unpack_field(ec, e2u, b1, 2)
        arrive(K_X2 + it, N8, x_refs)

        def correct(i, from_own):
            for c in range(3):
                pending = []
                for j in range(AY):
                    inner = from_own(j)
                    old = a2[c, i, j] if inner else xb[it, c, i, j]
                    keep = ex[i, j] > 0.0
                    e = e2u[c, (i + 1) // 2, (j + 1) // 2]
                    pending.append((j, jnp.where(keep, old + fx[i, j] * e, 0.0)))
                for j, val in pending:
                    a3[c, i, j] = val

        for i in range(AX):
            out = 0 if H <= i < H + NX else 1 if H - 1 <= i <= H + NX else 9
            correct(i, lambda j: out + (not H <= j < H + NY) + 9 * (not H - 1 <= j <= H + NY) < 2)
        smooth(a3, 1, *two_out, co1, w, rhs, bd, a4)
        smooth(a4, 1, *one_out, co1, w, rhs, ad, pv.at[it], 5)

        def keep_image(i, rows):
            return [(g, (it + 1, c, i, j), av) for j, vals in rows.items() for c, (_, av) in enumerate(vals)]

        sweep(pv.at[it], 1, *own, co1, w, keep_image, 4, False)

        q_refs = halo(g.at[1], g.at[1], 2)

        @pl.when(it == 0)
        def _():
            start(K_G + 1, N8, q_refs)

        def gram_plane(i, accs):
            accs = list(accs)
            for c in range(3):
                for j in range(H, H + NY):
                    left = [g[q, c, i, j] for q in range(2)] + [jnp.where(it == 1, g[2, c, i, j], 0.0)]
                    for k in range(NC):
                        right = row(pv[it, c, i, j, k : k + 1, :])
                        for q in range(3):
                            accs[q * NC + k] = accs[q * NC + k] + left[q] * right
            return tuple(accs)

        zeros = tuple(jnp.zeros((NC, NZ), F32) for _ in range(3 * NC))
        accs = lax.fori_loop(H, H + NX, gram_plane, zeros)
        out = jnp.zeros((NC, NZ), F32)
        for q in range(3):
            for k in range(NC):
                out = jnp.where(lanes() == q * NC + k, row(jnp.sum(accs[q * NC + k], axis=1, keepdims=True)), out)
        gram[it] = out

        @pl.when(it == 0)
        def _():
            drain(0)
            arrive(K_G + 1, N8, q_refs)
            sent(K_G + 1, N8, q_refs)

        return carry

    lax.fori_loop(0, 2, cycle, 0)

    def settle():
        drain(1)
        sent(K_E, N8, boxes(eb))
        sent(K_F, N8, boxes(fb))
        sent(K_G, N8, halo(raw, raw, 2))
        sent(K_E2, N14, e2_refs)

    def total(buffer, me, count, place, base, meanwhile=None):
        def copy(d):
            return pltpu.make_async_remote_copy(
                src_ref=buffer.at[me], dst_ref=buffer.at[me],
                send_sem=psend.at[base + d], recv_sem=precv.at[base + me],
                device_id=place(lax.rem(me + d, count)), device_id_type=MESH,
            )

        def landing(d):
            other = lax.rem(me + d, count)
            return pltpu.make_async_remote_copy(
                src_ref=buffer.at[other], dst_ref=buffer.at[other],
                send_sem=psend.at[base + d], recv_sem=precv.at[base + other],
                device_id=place(other), device_id_type=MESH,
            )

        for d in far_first(count):
            copy(d).start()
        if meanwhile is not None:
            meanwhile()
        for d in far_first(count)[::-1]:
            landing(d).wait_recv()
        for d in range(1, count):
            copy(d).wait_send()
        out = buffer[0]
        for k in range(1, count):
            out = out + buffer[k]
        return out

    grams = jnp.where(lanes() < 2 * NC, gram[0], pltpu.roll(gram[1], 2 * NC, 1))
    folded = jnp.where(lanes() < NZ // 2, grams, pltpu.roll(pltpu.roll(grams, NC // 2, 0), NZ // 2, 1))
    ps1[gy] = folded[: NC // 2]
    ps2[gx] = total(ps1, gy, size_y, lambda k: (gx, k), 0, settle)
    sums = total(ps2, gx, size_x, lambda k: (k, gy), size_y)
    sums = jnp.concatenate([sums, pltpu.roll(sums, NZ // 2, 1)], axis=0)

    rz = sums
    qp = up(sums, NC)
    ru = up(sums, 2 * NC)
    qu = up(sums, 3 * NC)
    wu = up(sums, 4 * NC)
    alpha = solve(columns(qp), rz)
    alpha_t = flipped(alpha)
    qua = mm(columns(qu), alpha)
    rz2 = rz - mm(columns(ru), alpha) + mm(alpha_t, qua - qp)
    mix = jnp.where(lanes() == subl(), 1.0, 0.0) + solve(columns(rz), rz2)
    ahead = mm(flipped(qp), mix) - qua
    behind = mm(flipped(wu), alpha) - mm(flipped(qu), mix)
    alpha2 = solve(columns(mm(flipped(mix), ahead) + mm(alpha_t, behind)), rz2)
    for q, m in enumerate((alpha + mm(columns(mix), alpha2), mm(columns(alpha), alpha2))):
        for k, col in enumerate(flipped(m)):
            mats[q, k] = col

    def finish(n, carry):
        c, x = lax.div(n, NX), lax.rem(n, NX)
        i = H + x
        for one, two, ref, base in ((pv.at[0], pv.at[1], stage.at[0], None), (g.at[1], g.at[2], stage.at[1], g.at[0])):
            accs = [None] * NY
            for k in range(NC):
                m1, m2 = mats[0, k], mats[1, k]
                for y in range(NY):
                    j = H + y
                    term = row(one[c, i, j, k : k + 1, :]) * m1 - row(two[c, i, j, k : k + 1, :]) * m2
                    accs[y] = term if k == 0 else accs[y] + term
            pending = [(y, acc if base is None else base[c, i, H + y] - acc) for y, acc in enumerate(accs)]
            for y, val in pending:
                ref[pl.ds((c * NC * NX + x) * NY + y, NC, stride=NX * NY), :] = val
        return carry

    stores = []
    for c in range(3):
        lax.fori_loop(c * NX, (c + 1) * NX, finish, 0)
        part = pl.ds(c * NC * NX * NY, NC * NX * NY)
        for q, ref in enumerate((xo, ro)):
            copy = pltpu.make_async_copy(stage.at[q, part], ref.at[part], stored.at[q, c])
            copy.start()
            stores.append(copy)
    for copy in stores:
        copy.wait()


def publish(a, b, out_a, out_b, stage, sem):
    loads, stores = [], []
    n = a.shape[0] // PIECES
    for k in range(PIECES):
        for q, (one, two) in enumerate(((a, out_a), (b, out_b))):
            at = pl.ds(k * n, n)
            loads.append(pltpu.make_async_copy(one.at[at], stage.at[q, at], sem.at[0, q, k]))
            stores.append(pltpu.make_async_copy(stage.at[q, at], two.at[at], sem.at[1, q, k]))
    for copy in loads:
        copy.start()
    for load, store in zip(loads, stores):
        load.wait()
        store.start()
    for copy in stores:
        copy.wait()


def on_device(size_x, size_y, source_field, density_class, fixed_mask, load_nodes, load_forces):
    rows = NROWS
    tile = (NC, NZ)

    def vm(*dims):
        return pltpu.VMEM(dims + tile, F32)

    def level(nx, ny):
        return [vm(nx, ny)] * 5 + [vm(3, nx, ny), vm(nx, ny), vm(nx, ny), vm(3, nx, ny), vm(3, nx, ny)]

    scratch = [
        pltpu.VMEM((3, 3, NX, NY, NZ), F32), pltpu.VMEM((3, 3, NX, NY, NZ), F32), vm(5, 3),
        vm(AX, AY), vm(AX, AY), vm(10, 12), vm(5, 6), vm(),
        vm(3, 3, AX, AY), vm(2, 3, AX, AY), vm(3, AX, AY), vm(3, AX, AY), vm(3, AX, AY), vm(3, AX, AY),
        vm(2, 3, AX, AY), vm(AX, AY), pltpu.VMEM((3 * 8 * 12 * NC + 4 * NC, NZ), F32),
    ]
    scratch += level(AX, AY) + level(6, 8) + level(5, 6)
    scratch += [vm(3, 2, 4), vm(2, 3, 3, 8), vm(2, 3, 3, 8), vm(2, 3, 3, 8)]
    scratch += [vm(3, 6, 8)] * 5 + [vm(6, 8), vm(3, 6, 8)]
    scratch += [vm(3, 1, 2), vm(2, 3, 5, 3), vm(3, 5, 6), vm(3, 5, 6), vm(3, 5, 6), vm(5, 6)]
    half = (NC // 2, NZ)
    scratch += [vm(2), pltpu.VMEM((size_y,) + half, F32), pltpu.VMEM((size_x,) + half, F32), vm(2, NC), vm(3, AX, AY), vm(3, NX, 4)]
    scratch += [pltpu.VMEM((AX, 16, NZ), F32)] * 2
    sems = pltpu.SemaphoreType.DMA
    scratch += [sems((KINDS, len(N14))), sems((KINDS, len(N14))), sems((size_x + size_y,)), sems((size_x + size_y,))]
    spare = NROWS + NX * NY
    scratch += [pltpu.VMEM((spare, NZ), F32), pltpu.VMEM((2, spare, NZ), F32), sems((2, 3))]
    scratch += [pltpu.VMEM(v.shape, v.dtype) for v in (density_class, fixed_mask, load_nodes, load_forces)]
    scratch += [sems((5,))]
    whole = pl.BlockSpec(memory_space=pl.ANY)
    shape = jax.ShapeDtypeStruct((rows, NZ), F32)
    sol, res = pl.pallas_call(
        functools.partial(kernel, size_x, size_y),
        out_shape=(shape, shape),
        in_specs=[whole] * 5,
        out_specs=(whole, whole),
        scratch_shapes=scratch,
        compiler_params=pltpu.CompilerParams(
            collective_id=0, has_side_effects=True, vmem_limit_bytes=56 * 1024 * 1024
        ),
        name="block_pcg",
    )(source_field.reshape(rows, NZ), density_class, fixed_mask, load_nodes, load_forces)
    sol, res = pl.pallas_call(
        publish,
        out_shape=(shape, shape),
        in_specs=[whole] * 2,
        out_specs=(whole, whole),
        scratch_shapes=[pltpu.VMEM((2, rows, NZ), F32), sems((2, 2, PIECES))],
        name="publish",
    )(sol, res)
    return sol.reshape(source_field.shape), res.reshape(source_field.shape)


def solution(mesh):
    placed = (P(None, None, "gx", "gy", None), P("gx", "gy", None), P("gx", "gy", None), P(), P())
    return jax.shard_map(
        functools.partial(on_device, mesh.shape["gx"], mesh.shape["gy"]),
        mesh=mesh,
        in_specs=placed,
        out_specs=(P(None, None, "gx", "gy", None), P(None, None, "gx", "gy", None)),
        check_vma=False,
    )
```

```python
import functools
import math

import jax
import jax.numpy as jnp
from jax import lax
from jax.experimental import pallas as pl
from jax.experimental.pallas import tpu as pltpu
from jax.sharding import PartitionSpec as P

CLASSES = 16
MU = 1.0 / 2.6
LAM = 0.3 / 0.52
MIN_MODULUS = 0.05
STEP_A = 1.0 / (2.7 + 2.1 * math.cos(math.pi / 4.0))
STEP_B = 1.0 / (2.7 - 2.1 * math.cos(math.pi / 4.0))
MESH = pl.DeviceIdType.MESH
F32 = jnp.float32

NX, NY, NC, NZ, LOADS = 4, 8, 8, 128, 64
NROWS = 3 * NC * NX * NY
H = 3
AX, AY = NX + 2 * H, NY + 2 * H
N8 = [(1, -1), (-1, 1), (1, 1), (-1, -1), (1, 0), (-1, 0), (0, 1), (0, -1)]
N14 = [(dx, dy) for dx in (2, -2, 1, -1, 0) for dy in (1, -1, 0) if (dx, dy) != (0, 0)]

K_E, K_F, K_E2, K_G, K_X2, K_G2, K_X2C, K_G3, K_EC = 0, 1, 2, 3, 5, 7, 9, 11, 13
KINDS = 15
PIECES = 4


def far_first(count):
    return sorted(range(1, count), key=lambda d: abs(d - count / 2))


def lanes():
    return lax.broadcasted_iota(jnp.int32, (NC, NZ), 1)


def subl():
    return lax.broadcasted_iota(jnp.int32, (NC, NZ), 0)


def up(v, s):
    return pltpu.roll(v, NZ - s, 1)


def down(v, s):
    return pltpu.roll(v, s, 1)


def pair_sum(v, s):
    other = jnp.where((lanes() & s) == 0, up(v, s), down(v, s))
    return v + other


def row(v):
    return jnp.broadcast_to(v, (NC, NZ))


def span(d, n, h, base):
    if d > 0:
        return n - h, base - h, h
    if d < 0:
        return 0, base + n, h
    return 0, base, n


def coefficients(s, e_at, f_at, low, inv, co, unroll=False):
    kx, ky, kzp, fup, dm, cw, cf, ff, ad, bd = co
    last = lanes() >= NZ - s
    first = lanes() < s
    half = 0.5 * MU

    def lower(i, carry):
        pending = []
        for j in range(*low[1]):
            e, f = e_at(i, j), f_at(i, j)
            fx, fy = f_at(i + 1, j), f_at(i, j + 1)
            fzp = jnp.where(last, 0.0, up(f, s))
            ezp = up(e, s)
            le = LAM * e
            hf = half * f
            pending += [
                (kx, (i, j), (e + e_at(i + 1, j)) * (hf * fx)),
                (ky, (i, j), (e + e_at(i, j + 1)) * (hf * fy)),
                (kzp, (i, j), (e + ezp) * (hf * fzp)),
                (fup, (i, j), fzp),
                (cw, (0, i, j), le * fx),
                (cw, (1, i, j), le * fy),
                (cw, (2, i, j), le * fzp),
                (cf, (i, j), le * f),
                (ff, (i, j), f),
            ]
            if j % 3 == 2 or j == low[1][1] - 1:
                for ref, idx, val in pending:
                    ref[idx] = val
                pending = []
        return carry

    loop(low[0][0], low[0][1], lower, unroll)

    def smoother(i, carry):
        pending = []
        for j in range(*inv[1]):
            e, f = e_at(i, j), f_at(i, j)
            ezp = jnp.where(last, 0.0, up(e, s))
            ezm = jnp.where(first, 0.0, down(e, s))
            ex, ey = e_at(i - 1, j), e_at(i, j - 1)
            d = half * (ex + e_at(i + 1, j) + ey + e_at(i, j + 1) + ezm + ezp + 6.0 * e)
            pending.append((dm, (i, j), f * d + (1.0 - f)))
            for c, below in enumerate((ex, ey, ezm)):
                diag = jnp.where(e > 0.0, d + LAM * (e + below), 1.0)
                dinv = jnp.where(e > 0.0, f / diag + (1.0 - f), 0.0)
                pending.append((ad, (c, i, j), STEP_A * dinv))
                pending.append((bd, (c, i, j), STEP_B * dinv))
            if j % 3 == 2 or j == inv[1][1] - 1:
                for ref, idx, val in pending:
                    ref[idx] = val
                pending = []
        return carry

    loop(inv[0][0], inv[0][1], smoother, unroll)


def compact_coefficients(e_ref, f_ref, co, ex, fx):
    kx, ky, kzp, fup, dm, cw, cf, ff, ad, bd = co
    half = 0.5 * MU
    wide = (16, NZ)
    lane = lax.broadcasted_iota(jnp.int32, wide, 1)

    def zup(v):
        return jnp.where(lane == NZ - 1, 0.0, pltpu.roll(v, NZ - 1, 1))

    def ynext(v):
        return pltpu.roll(v, 15, 0)

    def plane(i, carry):
        e, f, e1, f1 = e_ref[i], f_ref[i], e_ref[i + 1], f_ref[i + 1]
        fy, fz = ynext(f), zup(f)
        le, hf = LAM * e, half * f
        ahead = (
            (ex, (i,), e), (fx, (i,), f),
            (kx, (i,), (e + e1) * (hf * f1)),
            (ky, (i,), (e + ynext(e)) * (hf * fy)),
            (kzp, (i,), (e + zup(e)) * (hf * fz)),
            (fup, (i,), fz), (cw, (0, i), le * f1), (cw, (1, i), le * fy),
            (cw, (2, i), le * fz), (cf, (i,), le * f), (ff, (i,), f),
        )
        for ref, at, val in ahead:
            for j in range(AY):
                ref[at + (j,)] = row(val[j : j + 1, :])
        return carry

    lax.fori_loop(0, AX - 1, plane, 0)
    for ref, source in ((ex, e_ref), (fx, f_ref)):
        last = source[AX - 1]
        for j in range(AY):
            ref[AX - 1, j] = row(last[j : j + 1, :])

    def smoother(i, carry):
        e, f = e_ref[i], f_ref[i]
        ey = pltpu.roll(e, 1, 0)
        ez = jnp.where(lane == 0, 0.0, pltpu.roll(e, 1, 1))
        eb = e_ref[i - 1]
        d = half * (eb + e_ref[i + 1] + ey + ynext(e) + ez + zup(e) + 6.0 * e)
        out = [(dm, (i,), f * d + (1.0 - f))]
        for c, below in enumerate((eb, ey, ez)):
            diag = jnp.where(e > 0.0, d + LAM * (e + below), 1.0)
            dinv = jnp.where(e > 0.0, f / diag + (1.0 - f), 0.0)
            out += [(ad, (c, i), STEP_A * dinv), (bd, (c, i), STEP_B * dinv)]
        for ref, at, val in out:
            for j in range(1, AY - 1):
                ref[at + (j,)] = row(val[j : j + 1, :])
        return carry

    lax.fori_loop(1, AX - 1, smoother, 0)


def sweep(v, s, xr, yr, co, w, emit, chunk, unroll):
    kx, ky, kzp, fup, dm, cw, cf, ff = co[:8]

    def spread(i, j, centre, ahead_x, ahead_y, ahead_z):
        total = centre[0] + centre[1] + centre[2]
        return cw[0, i, j] * ahead_x + cw[1, i, j] * ahead_y + cw[2, i, j] * ahead_z - cf[i, j] * total

    def at(i, j):
        return [v[c, i, j] for c in range(3)]

    before = xr[0] - 1
    stores = []
    for j in range(*yr):
        centre = at(before, j)
        stores.append((j, spread(before, j, centre, v[0, before + 1, j], v[1, before, j + 1], up(centre[2], s))))
    for j, val in stores:
        w[before, j] = val

    def body(i, carry):
        j0 = yr[0] - 1
        prev = at(i, j0)
        here = at(i, yr[0])
        wprev = spread(i, j0, prev, v[0, i + 1, j0], here[1], up(prev[2], s))
        kyprev = ky[i, j0]
        for ja in range(yr[0], yr[1], chunk):
            rows, ws = {}, []
            for j in range(ja, min(ja + chunk, yr[1])):
                nxt = at(i, j + 1)
                ahead = [v[c, i + 1, j] for c in range(3)]
                zp = [up(here[c], s) for c in range(3)]
                wc = spread(i, j, here, ahead[0], nxt[1], zp[2])
                k = (kx[i, j], kx[i - 1, j], ky[i, j], kyprev, kzp[i, j])
                f, d = ff[i, j], dm[i, j]
                fwc = f * wc
                gain = (f * w[i - 1, j] - fwc, f * wprev - fwc, -fwc)
                out = []
                for c in range(3):
                    one = d * here[c] + gain[c]
                    two = k[0] * ahead[c] + k[1] * v[c, i - 1, j]
                    three = k[2] * nxt[c] + k[3] * prev[c]
                    back = k[4] * here[c]
                    if c == 2:
                        back = back - fup[i, j] * wc
                    out.append((here[c], (one - two) - (three + k[4] * zp[c]) - down(back, s)))
                rows[j] = out
                ws.append((j, wc))
                prev, here, wprev, kyprev = here, nxt, wc, k[2]
            pending = emit(i, rows)
            for j, val in ws:
                w[i, j] = val
            for ref, idx, val in pending:
                ref[idx] = val
        return carry

    loop(xr[0], xr[1], body, unroll)


def loop(lo, hi, body, unroll):
    if unroll:
        for i in range(lo, hi):
            body(i, 0)
    else:
        lax.fori_loop(lo, hi, body, 0)


def smooth(v, s, xr, yr, co, w, rhs, step, out, chunk=4, unroll=False):
    def emit(i, rows):
        return [
            (out, (c, i, j), vc + step[c, i, j] * (rhs[c, i, j] - av))
            for j, vals in rows.items()
            for c, (vc, av) in enumerate(vals)
        ]

    sweep(v, s, xr, yr, co, w, emit, chunk, unroll)


def restrict(v, s, xr, yr, co, w, rhs, part, coarse, unroll=False):
    def emit(i, rows):
        pending = []
        for j in list(rows)[::2]:
            for c in range(3):
                total = (rhs[c, i, j] - rows[j][c][1]) + (rhs[c, i, j + 1] - rows[j + 1][c][1])
                pending.append((part, (c, i - xr[0], (j - yr[0]) // 2), total))
        return pending

    sweep(v, s, xr, yr, co, w, emit, 4, unroll)
    pending = []
    for c in range(3):
        for q in range((xr[1] - xr[0]) // 2):
            for y2 in range((yr[1] - yr[0]) // 2):
                pending.append(((c, q, y2), pair_sum(part[c, 2 * q, y2] + part[c, 2 * q + 1, y2], s)))
    for idx, val in pending:
        coarse[idx] = val


def pick(m, k):
    return row(m[k : k + 1, :])


def columns(m):
    return [row(m[:, k : k + 1]) for k in range(NC)]


def flipped(m):
    diagonal = lanes() == subl()
    return [row(jnp.sum(jnp.where(diagonal, pick(m, k), 0.0), axis=1, keepdims=True)) for k in range(NC)]


def tree(terms):
    while len(terms) > 1:
        terms = [sum(terms[k : k + 2]) for k in range(0, len(terms), 2)]
    return terms[0]


def mm(cols, m):
    return tree([cols[k] * pick(m, k) for k in range(NC)])


def solve(cols, rhs):
    left = list(cols)
    for k in range(NC):
        pivot_row = subl() == k
        inverse = 1.0 / pick(left[k], k)
        for j in range(k + 1, NC):
            scaled = pick(left[j], k) * inverse
            left[j] = jnp.where(pivot_row, scaled, left[j] - left[k] * scaled)
        scaled = pick(rhs, k) * inverse
        rhs = jnp.where(pivot_row, scaled, rhs - left[k] * scaled)
    return rhs


def kernel(
    size_x, size_y,
    src, dens_in, mask_in, nodes_in, forces_in, xo, ro,
    eb, fb, e2b, ex, fx, e2x, e3x, one,
    g, pv, a1, a2, a3, a4, xb, w, loadbuf,
    kx, ky, kzp, fup, dm, cw, cf, ff, ad, bd,
    kx2, ky2, kzp2, fup2, dm2, cw2, cf2, ff2, ad2, bd2,
    kx3, ky3, kzp3, fup3, dm3, cw3, cf3, ff3, ad3, bd3,
    t2, g2r, x2r, ecr, g2u, b1, b2, b3, b4, w2, e2u,
    t3, g3r, g3u, c1, c2, w3,
    gram, ps1, ps2, mats, raw, pairs, ec0, fc0,
    send, recv, psend, precv, flat_src, stage, stored, dens, mask, nodes, forces, fetched,
):
    gx, gy = lax.axis_index("gx"), lax.axis_index("gy")
    co1 = (kx, ky, kzp, fup, dm, cw, cf, ff, ad, bd)
    co2 = (kx2, ky2, kzp2, fup2, dm2, cw2, cf2, ff2, ad2, bd2)
    co3 = (kx3, ky3, kzp3, fup3, dm3, cw3, cf3, ff3, ad3, bd3)
    even = (lanes() & 1) == 0
    low2 = (lanes() & 2) == 0

    def valid(dx, dy):
        return (gx + dx >= 0) & (gx + dx < size_x) & (gy + dy >= 0) & (gy + dy < size_y)

    def message(kind, k, d, refs):
        a, b = refs(*d)
        return pltpu.make_async_remote_copy(
            src_ref=a, dst_ref=b, send_sem=send.at[kind, k], recv_sem=recv.at[kind, k],
            device_id=(gx + d[0], gy + d[1]), device_id_type=MESH,
        )

    def start(kind, group, refs):
        for k, d in enumerate(group):
            @pl.when(valid(*d))
            def _():
                message(kind, k, d, refs).start()

    def arrive(kind, group, refs):
        for k, d in enumerate(group):
            @pl.when(valid(-d[0], -d[1]))
            def _():
                message(kind, k, d, refs).wait_recv()

    def sent(kind, group, refs):
        for k, d in enumerate(group):
            @pl.when(valid(*d))
            def _():
                message(kind, k, d, refs).wait_send()

    def boxes(ref):
        def refs(dx, dy):
            n = NX if dx == 0 else 2 if dx == dy else 3
            at = pl.ds(NX - n if dx > 0 else 0, n)
            return ref.at[1, 1, at], ref.at[1 - dx, 1 - dy, at]
        return refs

    def e2_refs(dx, dy):
        return e2b.at[2, 1], e2b.at[2 - dx, 1 - dy]

    def halo(source, target, h, skip=0):
        def side(d, other, n):
            if d == 0:
                return 0, H, n
            near, far = (skip, h) if other == 0 else (0, h - 1 if other == d else h)
            return (n - far, H - far, far - near) if d > 0 else (near, H + n + near, far - near)

        def refs(dx, dy):
            sx, tx, nx = side(dx, dy, NX)
            sy, ty, ny = side(dy, dx, NY)
            a = source.at[:, pl.ds(H + sx, nx), pl.ds(H + sy, ny)]
            return a, target.at[:, pl.ds(tx, nx), pl.ds(ty, ny)]
        return refs

    def coarse_refs(ref):
        def refs(dx, dy):
            sy, ty, ny = span(dy, 4, 1 if dx == dy else 2, 2)
            return ref.at[:, 1, pl.ds(2 + sy, ny)], ref.at[:, 1 - dx, pl.ds(ty, ny)]
        return refs

    def g3_refs(ref):
        return lambda dx, dy: (ref.at[:, 2, 1], ref.at[:, 2 - dx, 1 - dy])

    inputs = ((dens_in, dens), (mask_in, mask), (src, flat_src.at[pl.ds(0, NROWS)]), (nodes_in, nodes), (forces_in, forces))
    fetch = [pltpu.make_async_copy(a, b, fetched.at[k]) for k, (a, b) in enumerate(inputs)]
    for copy in fetch:
        copy.start()
    zero3 = jnp.zeros((NX, NY, NZ), F32)
    for bx in range(3):
        for by in range(3):
            eb[bx, by] = zero3
            fb[bx, by] = zero3
    for bx in range(5):
        for by in range(3):
            e2b[bx, by] = jnp.zeros((NC, NZ), F32)
    bar = pltpu.get_barrier_semaphore()
    corners = [(dx, dy) for dx in (1, -1, 2, -2) for dy in (1, -1)]
    peers = jnp.int32(size_x + size_y - 2)

    for d in far_first(size_x):
        pl.semaphore_signal(bar, inc=1, device_id=(lax.rem(gx + d, size_x), gy), device_id_type=MESH)
    for d in far_first(size_y):
        pl.semaphore_signal(bar, inc=1, device_id=(gx, lax.rem(gy + d, size_y)), device_id_type=MESH)
    for d in corners:
        peers = peers + jnp.where(valid(*d), 1, 0)

        @pl.when(valid(*d))
        def _():
            pl.semaphore_signal(bar, inc=1, device_id=(gx + d[0], gy + d[1]), device_id_type=MESH)
    fetch[0].wait()
    fetch[1].wait()
    for x in range(NX):
        rel = (dens[x].astype(F32) + 1.0) / CLASSES
        eb[1, 1, x] = MIN_MODULUS + (1.0 - MIN_MODULUS) * rel * rel * rel
        fb[1, 1, x] = 1.0 - mask[x].astype(F32)
    halves = []
    for q in range(2):
        t = eb[1, 1, 2 * q] + eb[1, 1, 2 * q + 1]
        halves.append(0.25 * pair_sum(t + pltpu.roll(t, NY - 1, 0), 1))
    e2b[2, 1] = jnp.where((subl() & 1) == 0, halves[0], pltpu.roll(halves[1], 1, 0))

    fetch[2].wait()
    for c in range(3):
        for x in range(NX):
            for y in range(NY):
                raw[c, H + x, H + y] = flat_src[pl.ds((c * NC * NX + x) * NY + y, NC, stride=NX * NY), :]

    pl.semaphore_wait(bar, peers)

    start(K_E, N8, boxes(eb))
    start(K_F, N8, boxes(fb))
    start(K_G, N8, halo(raw, raw, 2))
    start(K_E2, N14, e2_refs)

    def load_case(i, carry):
        node = nodes[pl.ds(i, 1), :]
        nz = lax.rem(node, NZ)
        nyx = lax.div(node, NZ)
        ny = lax.rem(nyx, size_y * NY) - gy * NY + 2
        nx = lax.div(nyx, size_y * NY) - gx * NX + 2
        hot = jnp.where(lax.broadcasted_iota(jnp.int32, (NZ, LOADS), 0) == nz, 1.0, 0.0)
        rows = lax.broadcasted_iota(jnp.int32, (16, LOADS), 0)
        parts = []
        for c in range(3):
            force = forces[c, pl.ds(i, 1), :]
            for x in range(8):
                parts.append(jnp.where((rows == ny) & (nx == x), force, 0.0))
        got = lax.dot_general(
            jnp.concatenate(parts, axis=0), hot, (((1,), (1,)), ((), ())),
            precision=lax.Precision.HIGHEST, preferred_element_type=F32,
        )
        for k in range(24):
            loadbuf[pl.ds(k * 96 + i, 8, stride=NC), :] = got[16 * k : 16 * k + 8]
            loadbuf[pl.ds(k * 96 + 64 + i, 4, stride=NC), :] = got[16 * k + 8 : 16 * k + 12]
        return carry

    fetch[3].wait()
    fetch[4].wait()
    lax.fori_loop(0, NC, load_case, 0)

    arrive(K_E, N8, boxes(eb))
    arrive(K_F, N8, boxes(fb))
    for i in range(AX):
        bx, xl = (i + 1) // 4, (i + 1) % 4
        for source, flat in ((eb, ec0), (fb, fc0)):
            flat[i, 0:3] = source[bx, 0, xl, 5:8]
            flat[i, 3:11] = source[bx, 1, xl]
            flat[i, 11:14] = source[bx, 2, xl, 0:3]
    compact_coefficients(ec0, fc0, co1, ex, fx)

    arrive(K_G, N8, halo(raw, raw, 2))

    def first_rhs(i, carry):
        for c in range(3):
            pending = []
            for j in range(1, 13):
                k = ((c * 8 + i - 1) * 12 + j - 1) * NC
                total = fx[i, j] * (raw[c, i, j] + loadbuf[pl.ds(pl.multiple_of(k, NC), NC), :])
                total = jnp.where(ex[i, j] > 0.0, total, 0.0)
                pending.append((j, total, ad[c, i, j] * total))
            for j, val, step in pending:
                g[0, c, i, j] = val
                a1[c, i, j] = step
        return carry

    lax.fori_loop(1, 9, first_rhs, 0)

    def unpack(p):
        return jnp.where(even, p, down(p, 1)), jnp.where(even, up(p, 1), p)

    def unpack_field(packed, out, own, base):
        for c in range(3):
            for bx in range(3):
                pending = []
                for j in range(1 if bx == 0 else 0, 7 if bx == 2 else 8):
                    inner = bx == 1 and 2 <= j < 6
                    both = [own[c, base + a, base + j - 2] for a in range(2)] if inner else unpack(packed[c, bx, j])
                    for a, val in enumerate(both):
                        i = 2 * bx + a
                        if not inner:
                            val = jnp.where(ad2[0, i, j] > 0.0, val, 0.0)
                        pending.append(((c, i, j), val))
                for idx, val in pending:
                    out[idx] = val

    def pack_field(field, base, packed):
        for c in range(3):
            for j in range(4):
                packed[c, 1, 2 + j] = jnp.where(even, field[c, base[0], base[1] + j], field[c, base[0] + 1, base[1] + j])

    def drain(it):
        sent(K_X2 + it, N8, halo(a2, xb.at[it], 3, 1))
        sent(K_G2 + it, N8, coarse_refs(g2r.at[it]))
        sent(K_X2C + it, N8, coarse_refs(x2r.at[it]))
        sent(K_G3 + it, N14, g3_refs(g3r.at[it]))
        sent(K_EC + it, N8, coarse_refs(ecr.at[it]))

    def cycle(it, carry):
        rhs = g.at[it]
        own = ((H, H + NX), (H, H + NY))
        one_out = ((H - 1, H + NX + 1), (H - 1, H + NY + 1))
        two_out = ((H - 2, H + NX + 2), (H - 2, H + NY + 2))
        x_refs = halo(a2, xb.at[it], 3, 1)
        g2, x2, ec, g3 = g2r.at[it], x2r.at[it], ecr.at[it], g3r.at[it]

        @pl.when(it == 1)
        def _():
            def clean(i, c2_):
                for c in range(3):
                    pending = [(j, jnp.where(ex[i, j] > 0.0, rhs[c, i, j], 0.0)) for j in range(1, 13)]
                    pending = [(j, val, ad[c, i, j] * val) for j, val in pending]
                    for j, val, step in pending:
                        rhs[c, i, j] = val
                        a1[c, i, j] = step
                return c2_
            lax.fori_loop(1, 9, clean, 0)

        smooth(a1, 1, *one_out, co1, w, rhs, bd, a2, 5)
        restrict(a2, 1, *own, co1, w, rhs, pairs, t2)
        pack_field(t2, (0, 0), g2)
        start(K_G2 + it, N8, coarse_refs(g2))

        @pl.when(it == 0)
        def _():
            arrive(K_E2, N14, e2_refs)
            for i in range(10):
                for j in range(12):
                    k = (j % 4) * 2 + i % 2
                    e2x[i, j] = row(e2b[i // 2, j // 4, k : k + 1, :])
            for i in range(5):
                for j in range(6):
                    t = e2x[2 * i, 2 * j] + e2x[2 * i + 1, 2 * j] + e2x[2 * i, 2 * j + 1] + e2x[2 * i + 1, 2 * j + 1]
                    e3x[i, j] = 0.25 * pair_sum(t, 2)
            one[...] = jnp.ones((NC, NZ), F32)
            coefficients(
                2, lambda i, j: e2x[i + 2, j + 2], lambda i, j: one[...],
                ((0, 5), (0, 7)), ((0, 6), (0, 8)), co2,
            )
            coefficients(
                4, lambda i, j: e3x[i, j], lambda i, j: one[...],
                ((0, 4), (0, 5)), ((1, 4), (1, 5)), co3,
            )

        arrive(K_G2 + it, N8, coarse_refs(g2))
        unpack_field(g2, g2u, t2, 0)
        for c in range(3):
            for i in range(6):
                pending = [(j, ad2[c, i, j] * g2u[c, i, j]) for j in range(8)]
                for j, val in pending:
                    b1[c, i, j] = val
        own2, out2 = ((2, 4), (2, 6)), ((1, 5), (1, 7))
        smooth(b1, 2, *out2, co2, w2, g2u, bd2, b2, 3)
        pack_field(b2, (2, 2), x2)
        start(K_X2C + it, N8, coarse_refs(x2))
        restrict(b2, 2, *own2, co2, w2, g2u, pairs, t3)
        for c in range(3):
            r0, r1 = t3[c, 0, 0], t3[c, 0, 1]
            s0, s1 = ad3[c, 2, 2] * r0, ad3[c, 2, 3] * r1
            g3[c, 2, 1] = jnp.where(low2, jnp.where(even, r0, r1), jnp.where(even, s0, s1))
        start(K_G3 + it, N14, g3_refs(g3))
        start(K_X2 + it, N8, x_refs)
        arrive(K_X2C + it, N8, coarse_refs(x2))
        unpack_field(x2, b3, b2, 2)
        arrive(K_G3 + it, N14, g3_refs(g3))
        for c in range(3):
            pending = []
            for bx in range(5):
                for by in range(3):
                    for a, q in enumerate(unpack(g3[c, bx, by])):
                        j = 2 * by + a
                        keep = e3x[bx, j] > 0.0
                        if 1 <= bx <= 3 and 1 <= j <= 4:
                            pending.append((g3u, (c, bx, j), jnp.where(keep, jnp.where(low2, q, down(q, 2)), 0.0)))
                        pending.append((c1, (c, bx, j), jnp.where(keep, jnp.where(low2, up(q, 2), q), 0.0)))
            for ref, idx, val in pending:
                ref[idx] = val
        smooth(c1, 4, (1, 4), (1, 5), co3, w3, g3u, bd3, c2, 4)

        def add_coarsest(n, c2_):
            c, i = lax.div(n, 6), lax.rem(n, 6)
            at = lax.div(i, 2) + 1
            pending = [(j, b3[c, i, j] + c2[c, at, j // 2 + 1]) for j in range(8)]
            for j, val in pending:
                b3[c, i, j] = val
            return c2_

        lax.fori_loop(0, 18, add_coarsest, 0)
        smooth(b3, 2, *out2, co2, w2, g2u, bd2, b4, 3)
        smooth(b4, 2, *own2, co2, w2, g2u, ad2, b1, 4)
        pack_field(b1, (2, 2), ec)
        start(K_EC + it, N8, coarse_refs(ec))
        arrive(K_EC + it, N8, coarse_refs(ec))
        unpack_field(ec, e2u, b1, 2)
        arrive(K_X2 + it, N8, x_refs)

        def correct(i, from_own):
            for c in range(3):
                pending = []
                for j in range(AY):
                    inner = from_own(j)
                    old = a2[c, i, j] if inner else xb[it, c, i, j]
                    keep = ex[i, j] > 0.0
                    e = e2u[c, (i + 1) // 2, (j + 1) // 2]
                    pending.append((j, jnp.where(keep, old + fx[i, j] * e, 0.0)))
                for j, val in pending:
                    a3[c, i, j] = val

        for i in range(AX):
            out = 0 if H <= i < H + NX else 1 if H - 1 <= i <= H + NX else 9
            correct(i, lambda j: out + (not H <= j < H + NY) + 9 * (not H - 1 <= j <= H + NY) < 2)
        smooth(a3, 1, *two_out, co1, w, rhs, bd, a4)
        smooth(a4, 1, *one_out, co1, w, rhs, ad, pv.at[it], 5)

        def keep_image(i, rows):
            return [(g, (it + 1, c, i, j), av) for j, vals in rows.items() for c, (_, av) in enumerate(vals)]

        sweep(pv.at[it], 1, *own, co1, w, keep_image, 4, False)

        q_refs = halo(g.at[1], g.at[1], 2)

        @pl.when(it == 0)
        def _():
            start(K_G + 1, N8, q_refs)

        def gram_plane(i, accs):
            accs = list(accs)
            for c in range(3):
                for j in range(H, H + NY):
                    left = [g[q, c, i, j] for q in range(2)] + [jnp.where(it == 1, g[2, c, i, j], 0.0)]
                    for k in range(NC):
                        right = row(pv[it, c, i, j, k : k + 1, :])
                        for q in range(3):
                            accs[q * NC + k] = accs[q * NC + k] + left[q] * right
            return tuple(accs)

        zeros = tuple(jnp.zeros((NC, NZ), F32) for _ in range(3 * NC))
        accs = lax.fori_loop(H, H + NX, gram_plane, zeros)
        out = jnp.zeros((NC, NZ), F32)
        for q in range(3):
            for k in range(NC):
                out = jnp.where(lanes() == q * NC + k, row(jnp.sum(accs[q * NC + k], axis=1, keepdims=True)), out)
        gram[it] = out

        @pl.when(it == 0)
        def _():
            drain(0)
            arrive(K_G + 1, N8, q_refs)
            sent(K_G + 1, N8, q_refs)

        return carry

    lax.fori_loop(0, 2, cycle, 0)

    def settle():
        drain(1)
        sent(K_E, N8, boxes(eb))
        sent(K_F, N8, boxes(fb))
        sent(K_G, N8, halo(raw, raw, 2))
        sent(K_E2, N14, e2_refs)

    def total(buffer, me, count, place, base, meanwhile=None):
        def copy(d):
            return pltpu.make_async_remote_copy(
                src_ref=buffer.at[me], dst_ref=buffer.at[me],
                send_sem=psend.at[base + d], recv_sem=precv.at[base + me],
                device_id=place(lax.rem(me + d, count)), device_id_type=MESH,
            )

        def landing(d):
            other = lax.rem(me + d, count)
            return pltpu.make_async_remote_copy(
                src_ref=buffer.at[other], dst_ref=buffer.at[other],
                send_sem=psend.at[base + d], recv_sem=precv.at[base + other],
                device_id=place(other), device_id_type=MESH,
            )

        for d in far_first(count):
            copy(d).start()
        if meanwhile is not None:
            meanwhile()
        for d in far_first(count)[::-1]:
            landing(d).wait_recv()
        for d in range(1, count):
            copy(d).wait_send()
        out = buffer[0]
        for k in range(1, count):
            out = out + buffer[k]
        return out

    grams = jnp.where(lanes() < 2 * NC, gram[0], pltpu.roll(gram[1], 2 * NC, 1))
    folded = jnp.where(lanes() < NZ // 2, grams, pltpu.roll(pltpu.roll(grams, NC // 2, 0), NZ // 2, 1))
    ps1[gy] = folded[: NC // 2]
    ps2[gx] = total(ps1, gy, size_y, lambda k: (gx, k), 0, settle)
    sums = total(ps2, gx, size_x, lambda k: (k, gy), size_y)
    sums = jnp.concatenate([sums, pltpu.roll(sums, NZ // 2, 1)], axis=0)

    rz = sums
    qp = up(sums, NC)
    ru = up(sums, 2 * NC)
    qu = up(sums, 3 * NC)
    wu = up(sums, 4 * NC)
    alpha = solve(columns(qp), rz)
    alpha_t = flipped(alpha)
    qua = mm(columns(qu), alpha)
    rz2 = rz - mm(columns(ru), alpha) + mm(alpha_t, qua - qp)
    mix = jnp.where(lanes() == subl(), 1.0, 0.0) + solve(columns(rz), rz2)
    ahead = mm(flipped(qp), mix) - qua
    behind = mm(flipped(wu), alpha) - mm(flipped(qu), mix)
    alpha2 = solve(columns(mm(flipped(mix), ahead) + mm(alpha_t, behind)), rz2)
    for q, m in enumerate((alpha + mm(columns(mix), alpha2), mm(columns(alpha), alpha2))):
        for k, col in enumerate(flipped(m)):
            mats[q, k] = col

    def finish(n, carry):
        c, x = lax.div(n, NX), lax.rem(n, NX)
        i = H + x
        for one, two, ref, base in ((pv.at[0], pv.at[1], stage.at[0], None), (g.at[1], g.at[2], stage.at[1], g.at[0])):
            accs = [None] * NY
            for k in range(NC):
                m1, m2 = mats[0, k], mats[1, k]
                for y in range(NY):
                    j = H + y
                    term = row(one[c, i, j, k : k + 1, :]) * m1 - row(two[c, i, j, k : k + 1, :]) * m2
                    accs[y] = term if k == 0 else accs[y] + term
            pending = [(y, acc if base is None else base[c, i, H + y] - acc) for y, acc in enumerate(accs)]
            for y, val in pending:
                ref[pl.ds((c * NC * NX + x) * NY + y, NC, stride=NX * NY), :] = val
        return carry

    stores = []
    for c in range(3):
        lax.fori_loop(c * NX, (c + 1) * NX, finish, 0)
        part = pl.ds(c * NC * NX * NY, NC * NX * NY)
        for q, ref in enumerate((xo, ro)):
            copy = pltpu.make_async_copy(stage.at[q, part], ref.at[part], stored.at[q, c])
            copy.start()
            stores.append(copy)
    for copy in stores:
        copy.wait()


def publish(a, b, out_a, out_b, stage, sem):
    loads, stores = [], []
    n = a.shape[0] // PIECES
    for k in range(PIECES):
        for q, (one, two) in enumerate(((a, out_a), (b, out_b))):
            at = pl.ds(k * n, n)
            loads.append(pltpu.make_async_copy(one.at[at], stage.at[q, at], sem.at[0, q, k]))
            stores.append(pltpu.make_async_copy(stage.at[q, at], two.at[at], sem.at[1, q, k]))
    for copy in loads:
        copy.start()
    for load, store in zip(loads, stores):
        load.wait()
        store.start()
    for copy in stores:
        copy.wait()


def on_device(size_x, size_y, source_field, density_class, fixed_mask, load_nodes, load_forces):
    rows = NROWS
    tile = (NC, NZ)

    def vm(*dims):
        return pltpu.VMEM(dims + tile, F32)

    def level(nx, ny):
        return [vm(nx, ny)] * 5 + [vm(3, nx, ny), vm(nx, ny), vm(nx, ny), vm(3, nx, ny), vm(3, nx, ny)]

    scratch = [
        pltpu.VMEM((3, 3, NX, NY, NZ), F32), pltpu.VMEM((3, 3, NX, NY, NZ), F32), vm(5, 3),
        vm(AX, AY), vm(AX, AY), vm(10, 12), vm(5, 6), vm(),
        vm(3, 3, AX, AY), vm(2, 3, AX, AY), vm(3, AX, AY), vm(3, AX, AY), vm(3, AX, AY), vm(3, AX, AY),
        vm(2, 3, AX, AY), vm(AX, AY), pltpu.VMEM((3 * 8 * 12 * NC + 4 * NC, NZ), F32),
    ]
    scratch += level(AX, AY) + level(6, 8) + level(5, 6)
    scratch += [vm(3, 2, 4), vm(2, 3, 3, 8), vm(2, 3, 3, 8), vm(2, 3, 3, 8)]
    scratch += [vm(3, 6, 8)] * 5 + [vm(6, 8), vm(3, 6, 8)]
    scratch += [vm(3, 1, 2), vm(2, 3, 5, 3), vm(3, 5, 6), vm(3, 5, 6), vm(3, 5, 6), vm(5, 6)]
    half = (NC // 2, NZ)
    scratch += [vm(2), pltpu.VMEM((size_y,) + half, F32), pltpu.VMEM((size_x,) + half, F32), vm(2, NC), vm(3, AX, AY), vm(3, NX, 4)]
    scratch += [pltpu.VMEM((AX, 16, NZ), F32)] * 2
    sems = pltpu.SemaphoreType.DMA
    scratch += [sems((KINDS, len(N14))), sems((KINDS, len(N14))), sems((size_x + size_y,)), sems((size_x + size_y,))]
    spare = NROWS + NX * NY
    scratch += [pltpu.VMEM((spare, NZ), F32), pltpu.VMEM((2, spare, NZ), F32), sems((2, 3))]
    scratch += [pltpu.VMEM(v.shape, v.dtype) for v in (density_class, fixed_mask, load_nodes, load_forces)]
    scratch += [sems((5,))]
    whole = pl.BlockSpec(memory_space=pl.ANY)
    shape = jax.ShapeDtypeStruct((rows, NZ), F32)
    sol, res = pl.pallas_call(
        functools.partial(kernel, size_x, size_y),
        out_shape=(shape, shape),
        in_specs=[whole] * 5,
        out_specs=(whole, whole),
        scratch_shapes=scratch,
        compiler_params=pltpu.CompilerParams(
            collective_id=0, has_side_effects=True, vmem_limit_bytes=56 * 1024 * 1024
        ),
        name="block_pcg",
    )(source_field.reshape(rows, NZ), density_class, fixed_mask, load_nodes, load_forces)
    sol, res = pl.pallas_call(
        publish,
        out_shape=(shape, shape),
        in_specs=[whole] * 2,
        out_specs=(whole, whole),
        scratch_shapes=[pltpu.VMEM((2, rows, NZ), F32), sems((2, 2, PIECES))],
        name="publish",
    )(sol, res)
    return sol.reshape(source_field.shape), res.reshape(source_field.shape)


def solution(mesh):
    placed = (P(None, None, "gx", "gy", None), P("gx", "gy", None), P("gx", "gy", None), P(), P())
    return jax.shard_map(
        functools.partial(on_device, mesh.shape["gx"], mesh.shape["gy"]),
        mesh=mesh,
        in_specs=placed,
        out_specs=(P(None, None, "gx", "gy", None), P(None, None, "gx", "gy", None)),
        check_vma=False,
    )
```
